256 devices in a mesh: ingest: 128 (over x, z, y), span: 2 (over core).
Axes of the slice: x: 4, y: 4, z: 8, core: 2. Of those that a mesh axis runs over, the one named last changes fastest.
Arguments:
- embeddings: bfloat16 [131072, 768], P(('ingest', 'span')), may hold values from -100 to 100
- cluster_id: int32 [131072], P(('ingest', 'span')), may hold values from 0 to 127, as said below
- rank: int32 [131072], P(('ingest', 'span')), may hold values from 0 to 131071, each once
Outputs:
- max_cosine: float32 [131072], P(('ingest', 'span'))
The draws below stay inside these ranges and needn't reach their ends.
Inputs may be any that keep to these rules, and one draw needn't show every extreme that they name: `cluster_id`: the 512 embeddings of each device name one cluster at most 8 times, and some cluster exactly 8 times. `rank`: every value once.
All inputs are finite; a program needn't handle non-finite values.
Results may differ from the reference program's by a relative error of at most 0.00054.
Values may be sent and summed in bfloat16 or wider, within the bound.
A program may use at most 64 MiB of HBM per device.

```python
import math
import jax
import jax.numpy as jnp
from jax import lax

D = 768
ROWS_DEV = 512
CAP = 8
NCLUST = 128
ROWS = 131072
DEVICES = 256


def assign_clusters(key):
    blocks = ROWS // ROWS_DEV
    first_key, second_key, third_key = jax.random.split(key, 3)
    heaviness = jax.random.randint(first_key, (NCLUST,), 0, 4)
    jitter = jax.random.randint(second_key, (blocks, NCLUST), 0, 65536)
    scores = (heaviness[None, :] * 65536 + jitter) * NCLUST + jnp.arange(NCLUST, dtype=jnp.int32)[None, :]
    ordering = jnp.argsort(-scores, axis=1).astype(jnp.int32)
    positions = jnp.arange(ROWS_DEV, dtype=jnp.int32)
    half_rows = ROWS_DEV // 2
    quarter = NCLUST // 4
    groups = jnp.where(positions < half_rows, positions // CAP, quarter + (positions - half_rows) % (NCLUST - quarter))
    shuffles = jax.vmap(lambda sub_key: jax.random.permutation(sub_key, ROWS_DEV))(jax.random.split(third_key, blocks))
    shuffled = groups[shuffles]
    chosen = jnp.take_along_axis(ordering, shuffled, axis=1)
    return chosen.reshape(ROWS).astype(jnp.int32)


def draw_cluster_id(key, part):
    clusters = assign_clusters(key)
    return clusters


def draw_embeddings(key, part):
    clusters = assign_clusters(key)
    key = jax.random.fold_in(key, 7)
    streams = jax.random.split(key, 5)
    centers = jax.random.normal(streams[0], (NCLUST, D), jnp.float32)
    noise = jax.random.normal(streams[1], (ROWS, D), jnp.float32)
    mixing = jnp.exp(jax.random.uniform(streams[2], (ROWS, 1), jnp.float32, math.log(0.3), math.log(3.0)))
    scaling = jnp.exp(jax.random.uniform(streams[3], (ROWS, 1), jnp.float32, math.log(0.5), math.log(5.0)))
    columns = jnp.exp(jax.random.uniform(streams[4], (1, D), jnp.float32, -0.7, 0.7))
    values = scaling * (mixing * centers[clusters] + noise) * columns
    return jnp.clip(values, -100.0, 100.0).astype(jnp.bfloat16)


def setup_inputs(seed: int = 0) -> dict:
    key_of = jax.random.split(jax.random.key(seed), 4)
    return {
        "embeddings": draw_embeddings(jax.random.fold_in(key_of[3], 71), 0),
        "cluster_id": draw_cluster_id(jax.random.fold_in(key_of[3], 71), 0),
        "rank": jax.random.permutation(key_of[2], ROWS).astype(jnp.int32),
    }


def normalize(embeddings):
    widened = embeddings.astype(jnp.float32)
    return (widened * lax.rsqrt(lax.optimization_barrier(jnp.sum(widened * widened, axis=1, keepdims=True)) + 1e-06)).astype(jnp.bfloat16)

def reference(embeddings, cluster_id, rank):
    normed = normalize(embeddings)
    window = DEVICES * CAP
    ordering = jnp.argsort(cluster_id, stable=True).astype(jnp.int32)
    sorted_ids = cluster_id[ordering]
    sorted_units = normed[ordering].astype(jnp.float32)
    sorted_rank = rank[ordering]
    starts = jnp.searchsorted(sorted_ids, jnp.arange(NCLUST, dtype=jnp.int32)).astype(jnp.int32)
    padded_units = jnp.concatenate([sorted_units, jnp.zeros((window, D), jnp.float32)], axis=0)
    padded_ids = jnp.concatenate([sorted_ids, jnp.full((window,), -1, jnp.int32)], axis=0)
    padded_rank = jnp.concatenate([sorted_rank, jnp.zeros((window,), jnp.int32)], axis=0)

    def visit_cluster(result, cluster):
        offset = starts[cluster]
        window_rows = lax.dynamic_slice_in_dim(padded_units, offset, window, 0)
        window_ids = lax.dynamic_slice_in_dim(padded_ids, offset, window, 0)
        window_rank = lax.dynamic_slice_in_dim(padded_rank, offset, window, 0)
        members = window_ids == cluster
        scores = jnp.dot(window_rows, window_rows.T, precision=lax.Precision.HIGHEST)
        earlier = members[None, :] & (window_rank[None, :] < window_rank[:, None])
        highest = lax.optimization_barrier(jnp.max(jnp.where(earlier, scores, -1.0), axis=1))
        previous = lax.dynamic_slice_in_dim(result, offset, window, 0)
        result = lax.dynamic_update_slice_in_dim(result, jnp.where(members, highest, previous).astype(result.dtype), offset, 0)
        return (result, None)
    result, _ = lax.scan(visit_cluster, jnp.full((ROWS + window,), -1.0, jnp.float32), jnp.arange(NCLUST, dtype=jnp.int32))
    return jnp.zeros((ROWS,), jnp.float32).at[ordering].set(result[:ROWS])
```

```python
import jax
import jax.numpy as jnp
from jax import lax
from jax.experimental import pallas as pl
from jax.experimental.pallas import tpu as pltpu
from jax.sharding import PartitionSpec as P

XS, ZS, YS = 4, 8, 4
PLANE = XS * YS
CAP = 8
BLOCK = PLANE * CAP
BEYOND = float(2**30)
MESH = pl.DeviceIdType.MESH
Z_OFFSETS = (0, 1, 7, 2, 6, 3, 5, 4)
f32, bf16, i32 = jnp.float32, jnp.bfloat16, jnp.int32


def contract_last(a, b):
    return lax.dot_general(a, b, (((1,), (1,)), ((), ())), preferred_element_type=f32)


def kernel(
    emb_hbm, cid_ref, rank_ref, out_ref,
    emb, normed, onehot, snd, zrcv, prcv, own, sib,
    rsnd, zrk, prk, rown, rsib, qrank, acc, res, pres, zres,
    emb_sem, z_send, z_recv, zr_send, zr_recv, p_send, p_recv, pr_send, pr_recv,
    loc, s_send, s_recv, sr_send, sr_recv, o1_send, o1_recv, o2_send, o2_recv, loc_small,
):
    rows = cid_ref.shape[1]
    width = emb.shape[1]
    half = width // 2
    me = lax.axis_index("ingest")
    core = lax.axis_index("span")
    x, z, y = me // (ZS * YS), (me // YS) % ZS, me % YS
    mine = x * YS + y

    def chip(px, pz, py):
        return (px * ZS + pz) * YS + py

    def z_peer(offset):
        return (chip(x, lax.rem(z + offset, ZS), y), core)

    def plane_peer(r):
        px, py = lax.rem(x + r // YS, XS), lax.rem(y + lax.rem(r, YS), YS)
        return px * YS + py, (chip(px, z, py), core)

    sibling = (me, 1 - core)

    load = pltpu.make_async_copy(emb_hbm, emb, emb_sem)
    load.start()
    barrier = pltpu.get_barrier_semaphore()
    for offset in range(1, ZS):
        pl.semaphore_signal(barrier, inc=1, device_id=z_peer(offset), device_id_type=MESH)

    def greet(r, carry):
        pl.semaphore_signal(barrier, inc=1, device_id=plane_peer(r)[1], device_id_type=MESH)
        return carry

    lax.fori_loop(1, PLANE, greet, 0)
    pl.semaphore_signal(barrier, inc=1, device_id=sibling, device_id_type=MESH)

    cid = cid_ref[...]
    cx, cz, cy = cid >> 5, (cid >> 2) & 7, cid & 3
    dz = (cz - z) & 7
    step_of = jnp.where(dz <= 4, 2 * dz - 1, 2 * (ZS - dz))
    step_of = jnp.where(dz == 0, 0, step_of)
    owner = step_of * PLANE + cx * YS + cy
    hot = lax.broadcasted_iota(i32, (ZS * PLANE, rows), 0) == owner
    hot_f = jnp.where(hot, 1.0, 0.0)
    onehot[...] = hot_f.astype(bf16)
    upper = lax.broadcasted_iota(i32, (rows, rows), 0) < lax.broadcasted_iota(i32, (rows, rows), 1)
    before = jnp.dot(onehot[...], jnp.where(upper, 1.0, 0.0).astype(bf16), preferred_element_type=f32)
    place = jnp.sum(hot_f * before, axis=0, keepdims=True).astype(i32)
    slot = owner * CAP + place
    lane = mine * CAP + place
    at_lane = lax.broadcasted_iota(i32, (128, rows), 0) == lane

    number = rank_ref[...] + 1
    table = jnp.zeros((ZS * PLANE, 128), f32)
    for shift in (0, 6, 12):
        digit = ((number >> shift) & 63).astype(f32)
        spread = jnp.where(at_lane, digit, 0.0).astype(bf16)
        table += contract_last(onehot[...], spread) * float(1 << shift)
    for t in range(ZS * PLANE):
        row = table[t : t + 1, :]
        if t < PLANE:
            zrk[0, t] = row
        else:
            rsnd[t // PLANE, t % PLANE] = row

    load.wait()
    wide = emb[...].astype(f32)
    scale = lax.rsqrt(jnp.sum(wide * wide, axis=1, keepdims=True) + 1e-06)
    normed[...] = (wide * scale).astype(bf16)

    def place_rows(first, count):
        span = count * BLOCK
        ids = lax.broadcasted_iota(i32, (span, rows), 0) + first * BLOCK
        pick = jnp.where(ids == slot, 1.0, 0.0).astype(bf16)
        placed = jnp.dot(pick, normed[...], preferred_element_type=f32)
        placed = placed.reshape(count * PLANE, CAP, width)
        paired = jnp.concatenate([placed[:, :, :half], placed[:, :, half:]], axis=1)
        snd[first : first + count] = paired.astype(bf16).reshape(count, PLANE, 2 * CAP, half)

    def send_z(j):
        pltpu.make_async_remote_copy(
            src_ref=snd.at[j], dst_ref=zrcv.at[j], send_sem=z_send, recv_sem=z_recv.at[j],
            device_id=z_peer(Z_OFFSETS[j]), device_id_type=MESH,
        ).start()

    def send_plane(source, j):
        def one(r, carry):
            q, device = plane_peer(r)
            pltpu.make_async_remote_copy(
                src_ref=source.at[j, q], dst_ref=prcv.at[j, mine], send_sem=p_send,
                recv_sem=p_recv.at[j], device_id=device, device_id_type=MESH,
            ).start()
            return carry

        lax.fori_loop(1, PLANE, one, 0)
        pltpu.make_async_copy(source.at[j, mine], prcv.at[j, mine], loc.at[j]).start()

    place_rows(1, 2)
    pl.semaphore_wait(barrier, ZS - 1 + PLANE - 1 + 1)
    for j in range(1, ZS):
        pltpu.make_async_remote_copy(
            src_ref=rsnd.at[j], dst_ref=zrk.at[j], send_sem=zr_send, recv_sem=zr_recv,
            device_id=z_peer(Z_OFFSETS[j]), device_id_type=MESH,
        ).start()
    send_z(1)
    send_z(2)
    place_rows(3, 2)
    send_z(3)
    send_z(4)
    place_rows(5, 2)
    send_z(5)
    send_z(6)
    place_rows(7, 1)
    send_z(7)
    place_rows(0, 1)
    send_plane(snd, 0)

    pltpu.make_async_copy(rsnd.at[pl.ds(1, ZS - 1)], zrk.at[pl.ds(1, ZS - 1)], zr_recv).wait()

    def rank_on(r, carry):
        q, device = plane_peer(r)
        pltpu.make_async_remote_copy(
            src_ref=zrk.at[:, q], dst_ref=prk.at[mine], send_sem=pr_send, recv_sem=pr_recv,
            device_id=device, device_id_type=MESH,
        ).start()
        return carry

    lax.fori_loop(1, PLANE, rank_on, 0)
    own_rank = pltpu.make_async_copy(zrk.at[:, mine], prk.at[mine], loc_small)
    own_rank.start()
    acc[...] = jnp.full(acc.shape, -1.0, f32)
    own_rank.wait()
    pltpu.make_async_copy(prk.at[pl.ds(0, PLANE - 1)], prk.at[pl.ds(0, PLANE - 1)], pr_recv).wait()
    found = jnp.sum(prk[...], axis=0)
    rown[...] = jnp.where(found == 0.0, BEYOND, found - 1.0)
    pltpu.make_async_remote_copy(
        src_ref=rown, dst_ref=rsib, send_sem=sr_send, recv_sem=sr_recv,
        device_id=sibling, device_id_type=MESH,
    ).start()
    for i in range(ZS):
        qrank[i] = jnp.transpose(jnp.broadcast_to(rown[i], (BLOCK, BLOCK)))

    def hand_over(j):
        blocks = prcv.at[j, pl.ds(0, PLANE - 1)]
        pltpu.make_async_copy(blocks, blocks, p_recv.at[j]).wait()
        pltpu.make_async_copy(prcv.at[j, mine], prcv.at[j, mine], loc.at[j]).wait()
        block = prcv[j].astype(f32)
        low = block[:, :CAP, :].reshape(BLOCK, half)
        high = block[:, CAP:, :].reshape(BLOCK, half)
        own[j] = jnp.concatenate([low, high], axis=1).astype(bf16)
        pltpu.make_async_remote_copy(
            src_ref=own.at[j], dst_ref=sib.at[j], send_sem=s_send, recv_sem=s_recv.at[j],
            device_id=sibling, device_id_type=MESH,
        ).start()

    def score(i, j):
        keys = jnp.concatenate([own[j], sib[j]], axis=0)
        scores = contract_last(own[i], keys)
        theirs = qrank[i]
        near = jnp.where(rown[j] < theirs, scores[:, :BLOCK], -1.0)
        far = jnp.where(rsib[j] < theirs, scores[:, BLOCK:], -1.0)
        acc[i] = jnp.maximum(acc[i], jnp.maximum(near, far))

    def scores_of(j):
        pltpu.make_async_copy(sib.at[j], sib.at[j], s_recv.at[j]).wait()
        if j == 0:
            pltpu.make_async_copy(rsib, rsib, sr_recv).wait()
        for i in range(j + 1):
            score(i, j)
        for k in range(j):
            score(j, k)

    hand_over(0)
    for j in range(1, ZS):
        pltpu.make_async_copy(zrcv.at[j], zrcv.at[j], z_recv.at[j]).wait()
        send_plane(zrcv, j)
        if j >= 2:
            hand_over(j - 1)
            scores_of(j - 2)
    scores_of(ZS - 2)
    hand_over(ZS - 1)
    scores_of(ZS - 1)

    for i in range(ZS):
        res[i] = jnp.max(jnp.transpose(acc[i]), axis=0, keepdims=True)

    def give_back(r, carry):
        _, device = plane_peer(r)
        pltpu.make_async_remote_copy(
            src_ref=res, dst_ref=pres.at[mine], send_sem=o1_send, recv_sem=o1_recv,
            device_id=device, device_id_type=MESH,
        ).start()
        return carry

    lax.fori_loop(1, PLANE, give_back, 0)
    own_res = pltpu.make_async_copy(res, pres.at[mine], loc_small)
    own_res.start()
    own_res.wait()
    pltpu.make_async_copy(pres.at[pl.ds(0, PLANE - 1)], pres.at[pl.ds(0, PLANE - 1)], o1_recv).wait()
    for j in range(1, ZS):
        pltpu.make_async_remote_copy(
            src_ref=pres.at[:, j], dst_ref=zres.at[j], send_sem=o2_send, recv_sem=o2_recv,
            device_id=z_peer(ZS - Z_OFFSETS[j]), device_id_type=MESH,
        ).start()
    own_last = pltpu.make_async_copy(pres.at[:, 0], zres.at[0], loc_small)
    own_last.start()
    own_last.wait()
    pltpu.make_async_copy(zres.at[pl.ds(1, ZS - 1)], zres.at[pl.ds(1, ZS - 1)], o2_recv).wait()
    back = jnp.concatenate([zres[j, q] for j in range(ZS) for q in range(PLANE)], axis=0)
    back = jnp.transpose(back)
    total = jnp.zeros((128, rows), f32)
    for _ in range(3):
        part = back.astype(bf16)
        total += jnp.dot(part, onehot[...], preferred_element_type=f32)
        back = back - part.astype(f32)
    out_ref[...] = jnp.sum(jnp.where(at_lane, total, 0.0), axis=0, keepdims=True)

    def drain(ref, sem):
        pltpu.make_async_copy(ref, ref, sem).wait()

    drain(snd.at[pl.ds(1, ZS - 1)], z_send)
    drain(rsnd.at[pl.ds(1, ZS - 1)], zr_send)
    drain(prcv.at[:, pl.ds(0, PLANE - 1)], p_send)
    drain(prk.at[pl.ds(0, PLANE - 1)], pr_send)
    drain(own, s_send)
    drain(rown, sr_send)
    drain(pres.at[pl.ds(0, PLANE - 1)], o1_send)
    drain(zres.at[pl.ds(1, ZS - 1)], o2_send)


def body(embeddings, cluster_id, rank):
    rows, width = embeddings.shape
    half = width // 2
    blocks = (ZS, PLANE, 2 * CAP, half)
    small = (ZS, PLANE, 1, 128)
    vmem = pltpu.VMEM
    dma = pltpu.SemaphoreType.DMA
    out = pl.pallas_call(
        kernel,
        out_shape=jax.ShapeDtypeStruct((1, rows), f32),
        in_specs=[
            pl.BlockSpec(memory_space=pl.ANY),
            pl.BlockSpec(memory_space=vmem),
            pl.BlockSpec(memory_space=vmem),
        ],
        out_specs=pl.BlockSpec(memory_space=vmem),
        scratch_shapes=[
            vmem((rows, width), bf16),
            vmem((rows, width), bf16),
            vmem((ZS * PLANE, rows), bf16),
            vmem(blocks, bf16),
            vmem(blocks, bf16),
            vmem(blocks, bf16),
            vmem((ZS, BLOCK, width), bf16),
            vmem((ZS, BLOCK, width), bf16),
            vmem(small, f32),
            vmem(small, f32),
            vmem((PLANE, ZS, 1, 128), f32),
            vmem((ZS, 1, 128), f32),
            vmem((ZS, 1, 128), f32),
            vmem((ZS, BLOCK, BLOCK), f32),
            vmem((ZS, BLOCK, BLOCK), f32),
            vmem((ZS, 1, 128), f32),
            vmem((PLANE, ZS, 1, 128), f32),
            vmem(small, f32),
            dma, dma, dma((ZS,)), dma, dma, dma, dma((ZS,)), dma, dma,
            dma((ZS,)), dma, dma((ZS,)), dma, dma, dma, dma, dma, dma, dma,
        ],
        compiler_params=pltpu.CompilerParams(
            collective_id=0, has_side_effects=True, vmem_limit_bytes=40 << 20
        ),
        name="exchange_and_score",
    )(embeddings, cluster_id.reshape(1, rows), rank.reshape(1, rows))
    return out.reshape(rows)


def solution(mesh):
    in_specs = (P(("ingest", "span"), None), P(("ingest", "span")), P(("ingest", "span")))
    out_specs = P(("ingest", "span"))
    return jax.shard_map(body, mesh=mesh, in_specs=in_specs, out_specs=out_specs, check_vma=False)
```

```python
import jax
import jax.numpy as jnp
from jax import lax
from jax.experimental import pallas as pl
from jax.experimental.pallas import tpu as pltpu
from jax.sharding import PartitionSpec as P

XS, ZS, YS = 4, 8, 4
PLANE = XS * YS
CAP = 8
BLOCK = PLANE * CAP
BEYOND = float(2**30)
MESH = pl.DeviceIdType.MESH
Z_OFFSETS = (0, 1, 7, 2, 6, 3, 5, 4)
f32, bf16, i32 = jnp.float32, jnp.bfloat16, jnp.int32


def contract_last(a, b):
    return lax.dot_general(a, b, (((1,), (1,)), ((), ())), preferred_element_type=f32)


def kernel(
    emb_hbm, cid_hbm, rank_hbm, out_ref,
    emb, cid_ref, rank_ref, normed, onehot, snd, zrcv, prcv, own, sib,
    rsnd, zrk, prk, rown, rsib, qrank, acc, res, pres, zres,
    emb_sem, cid_sem, rank_sem, z_send, z_recv, zr_send, zr_recv, p_send, p_recv, pr_send, pr_recv,
    loc, s_send, s_recv, sr_send, sr_recv, o1_send, o1_recv, o2_send, o2_recv, loc_small,
):
    rows = cid_ref.shape[1]
    width = emb.shape[1]
    half = width // 2
    me = lax.axis_index("ingest")
    core = lax.axis_index("span")
    x, z, y = me // (ZS * YS), (me // YS) % ZS, me % YS
    mine = x * YS + y

    def chip(px, pz, py):
        return (px * ZS + pz) * YS + py

    def z_peer(offset):
        return (chip(x, lax.rem(z + offset, ZS), y), core)

    def plane_peer(r):
        px, py = lax.rem(x + r // YS, XS), lax.rem(y + lax.rem(r, YS), YS)
        return px * YS + py, (chip(px, z, py), core)

    sibling = (me, 1 - core)

    load_cid = pltpu.make_async_copy(cid_hbm, cid_ref, cid_sem)
    load_cid.start()
    load = pltpu.make_async_copy(emb_hbm, emb, emb_sem)
    load.start()
    load_rank = pltpu.make_async_copy(rank_hbm, rank_ref, rank_sem)
    load_rank.start()
    barrier = pltpu.get_barrier_semaphore()
    for offset in range(1, ZS):
        pl.semaphore_signal(barrier, inc=1, device_id=z_peer(offset), device_id_type=MESH)

    def greet(r, carry):
        pl.semaphore_signal(barrier, inc=1, device_id=plane_peer(r)[1], device_id_type=MESH)
        return carry

    lax.fori_loop(1, PLANE, greet, 0)
    pl.semaphore_signal(barrier, inc=1, device_id=sibling, device_id_type=MESH)

    load_cid.wait()
    cid = cid_ref[...]
    cx, cz, cy = cid >> 5, (cid >> 2) & 7, cid & 3
    dz = (cz - z) & 7
    step_of = jnp.where(dz <= 4, 2 * dz - 1, 2 * (ZS - dz))
    step_of = jnp.where(dz == 0, 0, step_of)
    owner = step_of * PLANE + cx * YS + cy
    hot = lax.broadcasted_iota(i32, (ZS * PLANE, rows), 0) == owner
    hot_f = jnp.where(hot, 1.0, 0.0)
    onehot[...] = hot_f.astype(bf16)
    upper = lax.broadcasted_iota(i32, (rows, rows), 0) < lax.broadcasted_iota(i32, (rows, rows), 1)
    before = jnp.dot(onehot[...], jnp.where(upper, 1.0, 0.0).astype(bf16), preferred_element_type=f32)
    place = jnp.sum(hot_f * before, axis=0, keepdims=True).astype(i32)
    slot = owner * CAP + place
    lane = mine * CAP + place
    at_lane = lax.broadcasted_iota(i32, (128, rows), 0) == lane

    load.wait()
    wide = emb[...].astype(f32)
    scale = lax.rsqrt(jnp.sum(wide * wide, axis=1, keepdims=True) + 1e-06)
    normed[...] = (wide * scale).astype(bf16)

    def place_rows(first, count):
        span = count * BLOCK
        ids = lax.broadcasted_iota(i32, (span, rows), 0) + first * BLOCK
        pick = jnp.where(ids == slot, 1.0, 0.0).astype(bf16)
        placed = jnp.dot(pick, normed[...], preferred_element_type=f32)
        placed = placed.reshape(count * PLANE, CAP, width)
        paired = jnp.concatenate([placed[:, :, :half], placed[:, :, half:]], axis=1)
        snd[first : first + count] = paired.astype(bf16).reshape(count, PLANE, 2 * CAP, half)

    def send_z(j):
        pltpu.make_async_remote_copy(
            src_ref=snd.at[j], dst_ref=zrcv.at[j], send_sem=z_send, recv_sem=z_recv.at[j],
            device_id=z_peer(Z_OFFSETS[j]), device_id_type=MESH,
        ).start()

    def send_plane(source, j):
        def one(r, carry):
            q, device = plane_peer(r)
            pltpu.make_async_remote_copy(
                src_ref=source.at[j, q], dst_ref=prcv.at[j, mine], send_sem=p_send,
                recv_sem=p_recv.at[j], device_id=device, device_id_type=MESH,
            ).start()
            return carry

        lax.fori_loop(1, PLANE, one, 0)
        pltpu.make_async_copy(source.at[j, mine], prcv.at[j, mine], loc.at[j]).start()

    def rank_along():
        load_rank.wait()
        number = rank_ref[...] + 1
        table = jnp.zeros((ZS * PLANE, 128), f32)
        for shift in (0, 6, 12):
            digit = ((number >> shift) & 63).astype(f32)
            spread = jnp.where(at_lane, digit, 0.0).astype(bf16)
            table += contract_last(onehot[...], spread) * float(1 << shift)
        for t in range(ZS * PLANE):
            row = table[t : t + 1, :]
            if t < PLANE:
                zrk[0, t] = row
            else:
                rsnd[t // PLANE, t % PLANE] = row
        for j in range(1, ZS):
            pltpu.make_async_remote_copy(
                src_ref=rsnd.at[j], dst_ref=zrk.at[j], send_sem=zr_send, recv_sem=zr_recv,
                device_id=z_peer(Z_OFFSETS[j]), device_id_type=MESH,
            ).start()

    def rank_within():
        arrived = zrk.at[pl.ds(1, ZS - 1)]
        pltpu.make_async_copy(arrived, arrived, zr_recv).wait()

        def one(r, carry):
            q, device = plane_peer(r)
            pltpu.make_async_remote_copy(
                src_ref=zrk.at[:, q], dst_ref=prk.at[mine], send_sem=pr_send, recv_sem=pr_recv,
                device_id=device, device_id_type=MESH,
            ).start()
            return carry

        lax.fori_loop(1, PLANE, one, 0)
        pltpu.make_async_copy(zrk.at[:, mine], prk.at[mine], loc_small).start()

    def rank_done():
        pltpu.make_async_copy(prk.at[mine], prk.at[mine], loc_small).wait()
        others = prk.at[pl.ds(0, PLANE - 1)]
        pltpu.make_async_copy(others, others, pr_recv).wait()
        found = jnp.sum(prk[...], axis=0)
        rown[...] = jnp.where(found == 0.0, BEYOND, found - 1.0)
        pltpu.make_async_remote_copy(
            src_ref=rown, dst_ref=rsib, send_sem=sr_send, recv_sem=sr_recv,
            device_id=sibling, device_id_type=MESH,
        ).start()
        for i in range(ZS):
            qrank[i] = jnp.transpose(jnp.broadcast_to(rown[i], (BLOCK, BLOCK)))

    def hand_over(j):
        blocks = prcv.at[j, pl.ds(0, PLANE - 1)]
        pltpu.make_async_copy(blocks, blocks, p_recv.at[j]).wait()
        pltpu.make_async_copy(prcv.at[j, mine], prcv.at[j, mine], loc.at[j]).wait()
        block = prcv[j].astype(f32)
        low = block[:, :CAP, :].reshape(BLOCK, half)
        high = block[:, CAP:, :].reshape(BLOCK, half)
        own[j] = jnp.concatenate([low, high], axis=1).astype(bf16)
        pltpu.make_async_remote_copy(
            src_ref=own.at[j], dst_ref=sib.at[j], send_sem=s_send, recv_sem=s_recv.at[j],
            device_id=sibling, device_id_type=MESH,
        ).start()

    def score(i, j):
        keys = jnp.concatenate([own[j], sib[j]], axis=0)
        scores = contract_last(own[i], keys)
        theirs = qrank[i]
        near = jnp.where(rown[j] < theirs, scores[:, :BLOCK], -1.0)
        far = jnp.where(rsib[j] < theirs, scores[:, BLOCK:], -1.0)
        acc[i] = jnp.maximum(acc[i], jnp.maximum(near, far))

    def scores_of(j):
        pltpu.make_async_copy(sib.at[j], sib.at[j], s_recv.at[j]).wait()
        if j == 0:
            pltpu.make_async_copy(rsib, rsib, sr_recv).wait()
        for i in range(j + 1):
            score(i, j)
        for k in range(j):
            score(j, k)

    place_rows(1, 2)
    pl.semaphore_wait(barrier, ZS - 1 + PLANE - 1 + 1)
    send_z(1)
    send_z(2)
    rank_along()
    place_rows(3, 2)
    send_z(3)
    send_z(4)
    place_rows(5, 2)
    send_z(5)
    send_z(6)
    place_rows(7, 1)
    send_z(7)
    place_rows(0, 1)
    send_plane(snd, 0)
    acc[...] = jnp.full(acc.shape, -1.0, f32)

    meanwhile = {
        1: [],
        2: [rank_within],
        3: [lambda: hand_over(0)],
        4: [lambda: hand_over(1), rank_done],
        5: [lambda: hand_over(2), lambda: scores_of(0), lambda: scores_of(1)],
        6: [lambda: hand_over(3), lambda: scores_of(2), lambda: hand_over(4), lambda: scores_of(3)],
        7: [lambda: hand_over(5), lambda: scores_of(4), lambda: hand_over(6), lambda: scores_of(5),
            lambda: scores_of(6), lambda: hand_over(7), lambda: scores_of(7)],
    }
    for j in range(1, ZS):
        pltpu.make_async_copy(zrcv.at[j], zrcv.at[j], z_recv.at[j]).wait()
        send_plane(zrcv, j)
        for step in meanwhile[j]:
            step()

    for i in range(ZS):
        res[i] = jnp.max(jnp.transpose(acc[i]), axis=0, keepdims=True)

    def give_back(r, carry):
        _, device = plane_peer(r)
        pltpu.make_async_remote_copy(
            src_ref=res, dst_ref=pres.at[mine], send_sem=o1_send, recv_sem=o1_recv,
            device_id=device, device_id_type=MESH,
        ).start()
        return carry

    lax.fori_loop(1, PLANE, give_back, 0)
    own_res = pltpu.make_async_copy(res, pres.at[mine], loc_small)
    own_res.start()
    own_res.wait()
    pltpu.make_async_copy(pres.at[pl.ds(0, PLANE - 1)], pres.at[pl.ds(0, PLANE - 1)], o1_recv).wait()
    for j in range(1, ZS):
        pltpu.make_async_remote_copy(
            src_ref=pres.at[:, j], dst_ref=zres.at[j], send_sem=o2_send, recv_sem=o2_recv,
            device_id=z_peer(ZS - Z_OFFSETS[j]), device_id_type=MESH,
        ).start()
    own_last = pltpu.make_async_copy(pres.at[:, 0], zres.at[0], loc_small)
    own_last.start()
    own_last.wait()
    pltpu.make_async_copy(zres.at[pl.ds(1, ZS - 1)], zres.at[pl.ds(1, ZS - 1)], o2_recv).wait()
    back = jnp.concatenate([zres[j, q] for j in range(ZS) for q in range(PLANE)], axis=0)
    back = jnp.transpose(back)
    total = jnp.zeros((128, rows), f32)
    for _ in range(3):
        part = back.astype(bf16)
        total += jnp.dot(part, onehot[...], preferred_element_type=f32)
        back = back - part.astype(f32)
    out_ref[...] = jnp.sum(jnp.where(at_lane, total, 0.0), axis=0, keepdims=True)

    def drain(ref, sem):
        pltpu.make_async_copy(ref, ref, sem).wait()

    drain(snd.at[pl.ds(1, ZS - 1)], z_send)
    drain(rsnd.at[pl.ds(1, ZS - 1)], zr_send)
    drain(prcv.at[:, pl.ds(0, PLANE - 1)], p_send)
    drain(prk.at[pl.ds(0, PLANE - 1)], pr_send)
    drain(own, s_send)
    drain(rown, sr_send)
    drain(pres.at[pl.ds(0, PLANE - 1)], o1_send)
    drain(zres.at[pl.ds(1, ZS - 1)], o2_send)


def body(embeddings, cluster_id, rank):
    rows, width = embeddings.shape
    half = width // 2
    blocks = (ZS, PLANE, 2 * CAP, half)
    small = (ZS, PLANE, 1, 128)
    vmem = pltpu.VMEM
    dma = pltpu.SemaphoreType.DMA
    out = pl.pallas_call(
        kernel,
        out_shape=jax.ShapeDtypeStruct((1, rows), f32),
        in_specs=[
            pl.BlockSpec(memory_space=pltpu.HBM),
            pl.BlockSpec(memory_space=pltpu.HBM),
            pl.BlockSpec(memory_space=pltpu.HBM),
        ],
        out_specs=pl.BlockSpec(memory_space=vmem),
        scratch_shapes=[
            vmem((rows, width), bf16),
            vmem((1, rows), i32),
            vmem((1, rows), i32),
            vmem((rows, width), bf16),
            vmem((ZS * PLANE, rows), bf16),
            vmem(blocks, bf16),
            vmem(blocks, bf16),
            vmem(blocks, bf16),
            vmem((ZS, BLOCK, width), bf16),
            vmem((ZS, BLOCK, width), bf16),
            vmem(small, f32),
            vmem(small, f32),
            vmem((PLANE, ZS, 1, 128), f32),
            vmem((ZS, 1, 128), f32),
            vmem((ZS, 1, 128), f32),
            vmem((ZS, BLOCK, BLOCK), f32),
            vmem((ZS, BLOCK, BLOCK), f32),
            vmem((ZS, 1, 128), f32),
            vmem((PLANE, ZS, 1, 128), f32),
            vmem(small, f32),
            dma, dma, dma, dma, dma((ZS,)), dma, dma, dma, dma((ZS,)), dma, dma,
            dma((ZS,)), dma, dma((ZS,)), dma, dma, dma, dma, dma, dma, dma,
        ],
        compiler_params=pltpu.CompilerParams(
            collective_id=0, has_side_effects=True, vmem_limit_bytes=40 << 20
        ),
        name="exchange_and_score",
    )(embeddings, cluster_id.reshape(1, rows), rank.reshape(1, rows))
    return out.reshape(rows)


def solution(mesh):
    in_specs = (P(("ingest", "span"), None), P(("ingest", "span")), P(("ingest", "span")))
    out_specs = P(("ingest", "span"))
    return jax.shard_map(body, mesh=mesh, in_specs=in_specs, out_specs=out_specs, check_vma=False)
```

```python
import jax
import jax.numpy as jnp
from jax import lax
from jax.experimental import pallas as pl
from jax.experimental.pallas import tpu as pltpu
from jax.sharding import PartitionSpec as P

XS, ZS, YS = 4, 8, 4
PLANE = XS * YS
CAP = 8
BLOCK = PLANE * CAP
BEYOND = float(2**30)
MESH = pl.DeviceIdType.MESH
Z_OFFSETS = (0, 1, 7, 2, 6, 3, 5, 4)
UNITS = tuple((j, 0, PLANE) for j in range(ZS - 1)) + ((ZS - 1, 0, PLANE // 2), (ZS - 1, PLANE // 2, PLANE))
f32, bf16, i32 = jnp.float32, jnp.bfloat16, jnp.int32


def contract_last(a, b):
    return lax.dot_general(a, b, (((1,), (1,)), ((), ())), preferred_element_type=f32)


def kernel(
    emb_hbm, cid_hbm, rank_hbm, out_ref,
    emb, cid_ref, rank_ref, normed, onehot, snd, zrcv, prcv, own, sib,
    rsnd, prk, rmid, rraw, rown, rsib, key_rank, acc, res, zres, zmid, fin,
    emb_sem, cid_sem, rank_sem, z_send, z_recv, p_send, p_recv, s_send, s_recv,
    r1_send, r1_recv, r2_send, r2_recv, r3_send, r3_recv, o1_send, o1_recv, o2_send, o2_recv,
):
    rows = cid_ref.shape[1]
    width = emb.shape[1]
    half = width // 2
    me = lax.axis_index("ingest")
    core = lax.axis_index("span")
    x, z, y = me // (ZS * YS), (me // YS) % ZS, me % YS

    def chip(px, pz, py):
        return (px * ZS + pz) * YS + py

    def z_peer(offset):
        return (chip(x, lax.rem(z + offset, ZS), y), core)

    def plane_peer(r):
        return (chip(lax.rem(x + r // YS, XS), z, lax.rem(y + r % YS, YS)), core)

    def plane_back(r):
        return (chip(lax.rem(x + XS - r // YS, XS), z, lax.rem(y + YS - r % YS, YS)), core)

    sibling = (me, 1 - core)

    def send(src, dst, send_sem, recv_sem, device):
        pltpu.make_async_remote_copy(
            src_ref=src, dst_ref=dst, send_sem=send_sem, recv_sem=recv_sem,
            device_id=device, device_id_type=MESH,
        ).start()

    def wait_for(ref, sem):
        pltpu.make_async_copy(ref, ref, sem).wait()

    load_cid = pltpu.make_async_copy(cid_hbm, cid_ref, cid_sem)
    load_cid.start()
    load = pltpu.make_async_copy(emb_hbm, emb, emb_sem)
    load.start()
    load_rank = pltpu.make_async_copy(rank_hbm, rank_ref, rank_sem)
    load_rank.start()
    barrier = pltpu.get_barrier_semaphore()
    for offset in range(1, ZS):
        pl.semaphore_signal(barrier, inc=1, device_id=z_peer(offset), device_id_type=MESH)
    for r in range(1, PLANE):
        pl.semaphore_signal(barrier, inc=1, device_id=plane_peer(r), device_id_type=MESH)
    pl.semaphore_signal(barrier, inc=1, device_id=sibling, device_id_type=MESH)

    load_cid.wait()
    cid = cid_ref[...]
    cx, cz, cy = cid >> 5, (cid >> 2) & 7, cid & 3
    dz = (cz - z) & 7
    step = jnp.where(dz <= 4, 2 * dz - 1, 2 * (ZS - dz))
    step = jnp.where(dz == 0, 0, step)
    across = ((cx - x) & 3) * YS + ((cy - y) & 3)
    hot = lax.broadcasted_iota(i32, (ZS * PLANE, rows), 0) == across * ZS + step
    hot_f = jnp.where(hot, 1.0, 0.0)
    onehot[...] = hot_f.astype(bf16)
    upper = lax.broadcasted_iota(i32, (rows, rows), 0) < lax.broadcasted_iota(i32, (rows, rows), 1)
    before = jnp.dot(onehot[...], jnp.where(upper, 1.0, 0.0).astype(bf16), preferred_element_type=f32)
    place = jnp.sum(hot_f * before, axis=0, keepdims=True).astype(i32)
    lane = across * CAP + place
    slot = step * BLOCK + lane
    at_lane = lax.broadcasted_iota(i32, (128, rows), 0) == lane

    load.wait()
    wide = emb[...].astype(f32)
    scale = lax.rsqrt(jnp.sum(wide * wide, axis=1, keepdims=True) + 1e-06)
    normed[...] = (wide * scale).astype(bf16)

    def place_rows(first, count):
        span = count * BLOCK
        ids = lax.broadcasted_iota(i32, (span, rows), 0) + first * BLOCK
        pick = jnp.where(ids == slot, 1.0, 0.0).astype(bf16)
        placed = jnp.dot(pick, normed[...], preferred_element_type=f32)
        placed = placed.reshape(count * PLANE, CAP, width)
        paired = jnp.concatenate([placed[:, :, :half], placed[:, :, half:]], axis=1)
        snd[first : first + count] = paired.astype(bf16).reshape(count, PLANE, 2 * CAP, half)

    def source(j):
        return snd if j == 0 else zrcv

    def send_z(u):
        j, lo, hi = UNITS[u]
        some = pl.ds(lo, hi - lo)
        send(snd.at[j, some], zrcv.at[j, some], z_send, z_recv.at[u], z_peer(Z_OFFSETS[j]))

    def send_plane(u):
        j, lo, hi = UNITS[u]
        for r in range(max(lo, 1), hi):
            send(source(j).at[j, r], prcv.at[j, r], p_send, p_recv.at[u], plane_peer(r))

    def rank_within():
        load_rank.wait()
        number = rank_ref[...] + 1
        table = jnp.zeros((ZS * PLANE, 128), f32)
        for shift in (0, 6, 12):
            digit = ((number >> shift) & 63).astype(f32)
            spread = jnp.where(at_lane, digit, 0.0).astype(bf16)
            table += contract_last(onehot[...], spread) * float(1 << shift)
        rsnd[...] = table.reshape(PLANE, ZS, 128)
        for r in range(1, PLANE):
            send(rsnd.at[r], prk.at[r], r1_send, r1_recv, plane_peer(r))

    def rank_along():
        wait_for(prk.at[pl.ds(1, PLANE - 1)], r1_recv)
        found = rsnd[0] + jnp.sum(prk[1:], axis=0)
        for j in range(ZS):
            rmid[j] = found[j : j + 1]
        for j in range(1, ZS):
            send(rmid.at[j], rraw.at[j], r2_send, r2_recv, z_peer(Z_OFFSETS[j]))

    def spread_ranks(ranks, base):
        for j in range(ZS):
            key_rank[base + j] = jnp.transpose(jnp.broadcast_to(ranks[j], (BLOCK, BLOCK)))

    def rank_done():
        wait_for(rraw.at[pl.ds(1, ZS - 1)], r2_recv)
        for j in range(ZS):
            found = rmid[0] if j == 0 else rraw[j]
            rown[j] = jnp.where(found == 0.0, BEYOND, found - 1.0)
        send(rown, rsib, r3_send, r3_recv, sibling)
        spread_ranks(rown, 0)

    def rank_sibling():
        wait_for(rsib, r3_recv)
        spread_ranks(rsib, ZS)

    def hand_over(u):
        j, lo, hi = UNITS[u]
        first = max(lo, 1)
        wait_for(prcv.at[j, pl.ds(first, hi - first)], p_recv.at[u])
        block = prcv[j, first:hi]
        if lo == 0:
            block = jnp.concatenate([source(j)[j, 0:1], block], axis=0)
        block = block.astype(f32)
        size = (hi - lo) * CAP
        low = block[:, :CAP, :].reshape(size, half)
        high = block[:, CAP:, :].reshape(size, half)
        own[j, lo * CAP : hi * CAP] = jnp.concatenate([low, high], axis=1).astype(bf16)
        some = pl.ds(lo * CAP, size)
        send(own.at[j, some], sib.at[j, some], s_send, s_recv.at[u], sibling)

    def score(keys, ranks, queries):
        first, count = queries
        wanted = own[first : first + count].reshape(count * BLOCK, width)
        scores = contract_last(keys, wanted)
        for i in range(count):
            part = scores[:, i * BLOCK : (i + 1) * BLOCK]
            part = jnp.where(ranks < rown[first + i], part, -1.0)
            best = jnp.max(part.reshape(-1, 8, BLOCK), axis=0)
            acc[first + i] = jnp.maximum(acc[first + i], best)

    def keys_of(j, lo, hi):
        span = slice(lo * CAP, hi * CAP)
        keys = jnp.concatenate([own[j, span], sib[j, span]], axis=0)
        ranks = jnp.concatenate([key_rank[j, span], key_rank[ZS + j, span]], axis=0)
        return keys, ranks

    def scores_of(u):
        j, lo, hi = UNITS[u]
        some = sib.at[j, pl.ds(lo * CAP, (hi - lo) * CAP)]
        wait_for(some, s_recv.at[u])
        keys, ranks = keys_of(j, lo, hi)
        last = j + 1 if hi - lo == PLANE else j
        for i in range(0, last, 2):
            score(keys, ranks, (i, min(2, last - i)))
        if hi == PLANE:
            for k in range(j + 1 if last == j else j):
                score(*keys_of(k, 0, PLANE), (j, 1))

    place_rows(1, 2)
    pl.semaphore_wait(barrier, ZS - 1 + PLANE - 1 + 1)
    send_z(1)
    send_z(2)
    rank_within()
    place_rows(3, 2)
    send_z(3)
    send_z(4)
    place_rows(5, 2)
    send_z(5)
    send_z(6)
    place_rows(7, 1)
    send_z(7)
    send_z(8)
    place_rows(0, 1)
    send_plane(0)
    acc[...] = jnp.full(acc.shape, -1.0, f32)
    rank_along()

    meanwhile = {
        1: [],
        2: [rank_done, (hand_over, 0)],
        3: [],
        4: [rank_sibling, (hand_over, 1), (hand_over, 2), (scores_of, 0)],
        5: [(scores_of, 1), (scores_of, 2)],
        6: [(hand_over, 3), (hand_over, 4), (scores_of, 3), (scores_of, 4)],
        7: [(hand_over, 5), (hand_over, 6), (scores_of, 5)],
        8: [(scores_of, 6), (hand_over, 7), (scores_of, 7), (hand_over, 8), (scores_of, 8)],
    }
    for u in range(1, len(UNITS)):
        j, lo, hi = UNITS[u]
        wait_for(zrcv.at[j, pl.ds(lo, hi - lo)], z_recv.at[u])
        send_plane(u)
        for task in meanwhile[u]:
            if isinstance(task, tuple):
                task[0](task[1])
            else:
                task()

    for j in range(ZS):
        res[j] = jnp.max(acc[j], axis=0, keepdims=True)
    for j in range(1, ZS):
        send(res.at[j], zres.at[j], o1_send, o1_recv, z_peer(ZS - Z_OFFSETS[j]))
    wait_for(zres.at[pl.ds(1, ZS - 1)], o1_recv)
    zmid[...] = jnp.concatenate([res[0]] + [zres[j] for j in range(1, ZS)], axis=0)
    for r in range(1, PLANE):
        send(zmid, fin.at[r], o2_send, o2_recv, plane_back(r))
    at_step = lax.broadcasted_iota(i32, (ZS, rows), 0) == step
    place_of = jnp.where(at_lane, 1.0, 0.0).astype(bf16)
    wait_for(fin.at[pl.ds(1, PLANE - 1)], o2_recv)
    group = lax.broadcasted_iota(i32, (ZS, 128), 1) // CAP
    back = jnp.where(group == 0, zmid[...], 0.0)
    for r in range(1, PLANE):
        back = jnp.where(group == r, fin[r], back)
    total = jnp.zeros((ZS, rows), f32)
    for _ in range(3):
        part = back.astype(bf16)
        total += jnp.dot(part, place_of, preferred_element_type=f32)
        back = back - part.astype(f32)
    out_ref[...] = jnp.sum(jnp.where(at_step, total, 0.0), axis=0, keepdims=True)

    wait_for(snd.at[pl.ds(1, ZS - 1)], z_send)
    wait_for(prcv.at[:, pl.ds(1, PLANE - 1)], p_send)
    wait_for(own, s_send)
    wait_for(prk.at[pl.ds(1, PLANE - 1)], r1_send)
    wait_for(rraw.at[pl.ds(1, ZS - 1)], r2_send)
    wait_for(rown, r3_send)
    wait_for(zres.at[pl.ds(1, ZS - 1)], o1_send)
    wait_for(fin.at[pl.ds(1, PLANE - 1)], o2_send)


def body(embeddings, cluster_id, rank):
    rows, width = embeddings.shape
    half = width // 2
    blocks = (ZS, PLANE, 2 * CAP, half)
    vmem = pltpu.VMEM
    dma = pltpu.SemaphoreType.DMA
    out = pl.pallas_call(
        kernel,
        out_shape=jax.ShapeDtypeStruct((1, rows), f32),
        in_specs=[pl.BlockSpec(memory_space=pltpu.HBM)] * 3,
        out_specs=pl.BlockSpec(memory_space=vmem),
        scratch_shapes=[
            vmem((rows, width), bf16),
            vmem((1, rows), i32),
            vmem((1, rows), i32),
            vmem((rows, width), bf16),
            vmem((ZS * PLANE, rows), bf16),
            vmem(blocks, bf16),
            vmem(blocks, bf16),
            vmem(blocks, bf16),
            vmem((ZS, BLOCK, width), bf16),
            vmem((ZS, BLOCK, width), bf16),
            vmem((PLANE, ZS, 128), f32),
            vmem((PLANE, ZS, 128), f32),
            vmem((ZS, 1, 128), f32),
            vmem((ZS, 1, 128), f32),
            vmem((ZS, 1, 128), f32),
            vmem((ZS, 1, 128), f32),
            vmem((2 * ZS, BLOCK, BLOCK), f32),
            vmem((ZS, 8, BLOCK), f32),
            vmem((ZS, 1, 128), f32),
            vmem((ZS, 1, 128), f32),
            vmem((ZS, 128), f32),
            vmem((PLANE, ZS, 128), f32),
            dma, dma, dma, dma, dma((len(UNITS),)), dma, dma((len(UNITS),)), dma, dma((len(UNITS),)),
            dma, dma, dma, dma, dma, dma, dma, dma, dma, dma,
        ],
        compiler_params=pltpu.CompilerParams(
            collective_id=0, has_side_effects=True, vmem_limit_bytes=62 << 20
        ),
        name="exchange_and_score",
    )(embeddings, cluster_id.reshape(1, rows), rank.reshape(1, rows))
    return out.reshape(rows)


def solution(mesh):
    in_specs = (P(("ingest", "span"), None), P(("ingest", "span")), P(("ingest", "span")))
    out_specs = P(("ingest", "span"))
    return jax.shard_map(body, mesh=mesh, in_specs=in_specs, out_specs=out_specs, check_vma=False)
```

```python
import jax
import jax.numpy as jnp
from jax import lax
from jax.experimental import pallas as pl
from jax.experimental.pallas import tpu as pltpu
from jax.sharding import PartitionSpec as P

XS, ZS, YS = 4, 8, 4
PLANE = XS * YS
CAP = 8
BLOCK = PLANE * CAP
BEYOND = float(2**30)
MESH = pl.DeviceIdType.MESH
Z_OFFSETS = (0, 1, 7, 2, 6, 3, 5, 4)
LAST = ZS - 1
EARLY = 5
UNITS = tuple((j, 0, PLANE) for j in range(ZS - 1)) + ((ZS - 1, 0, PLANE // 2), (ZS - 1, PLANE // 2, PLANE))
f32, bf16, i32 = jnp.float32, jnp.bfloat16, jnp.int32


def contract_last(a, b):
    return lax.dot_general(a, b, (((1,), (1,)), ((), ())), preferred_element_type=f32)


def kernel(
    emb_hbm, cid_hbm, rank_hbm, out_ref,
    emb, cid_ref, rank_ref, normed, onehot, snd, early, zrcv, prcv, own, sib,
    rsnd, zrk, rmid, prk, rown, rsib, key_rank, acc, res, zres, zmid, fin,
    emb_sem, cid_sem, rank_sem, z_send, z_recv, p_send, p_recv, e_send, e_recv, s_send, s_recv,
    r1_send, r1_recv, r2_send, r2_recv, r3_send, r3_recv, o1_send, o1_recv, o2_send, o2_recv,
):
    rows = cid_ref.shape[1]
    width = emb.shape[1]
    half = width // 2
    me = lax.axis_index("ingest")
    core = lax.axis_index("span")
    x, z, y = me // (ZS * YS), (me // YS) % ZS, me % YS

    def chip(px, pz, py):
        return (px * ZS + pz) * YS + py

    def z_peer(offset):
        return (chip(x, lax.rem(z + offset, ZS), y), core)

    def plane_peer(r):
        return (chip(lax.rem(x + r // YS, XS), z, lax.rem(y + r % YS, YS)), core)

    def plane_back(r):
        return (chip(lax.rem(x + XS - r // YS, XS), z, lax.rem(y + YS - r % YS, YS)), core)

    sibling = (me, 1 - core)

    def send(src, dst, send_sem, recv_sem, device):
        pltpu.make_async_remote_copy(
            src_ref=src, dst_ref=dst, send_sem=send_sem, recv_sem=recv_sem,
            device_id=device, device_id_type=MESH,
        ).start()

    def wait_for(ref, sem):
        pltpu.make_async_copy(ref, ref, sem).wait()

    load_cid = pltpu.make_async_copy(cid_hbm, cid_ref, cid_sem)
    load_cid.start()
    load = pltpu.make_async_copy(emb_hbm, emb, emb_sem)
    load.start()
    load_rank = pltpu.make_async_copy(rank_hbm, rank_ref, rank_sem)
    load_rank.start()
    barrier = pltpu.get_barrier_semaphore()
    for offset in range(1, ZS):
        pl.semaphore_signal(barrier, inc=1, device_id=z_peer(offset), device_id_type=MESH)
    for r in range(1, PLANE):
        pl.semaphore_signal(barrier, inc=1, device_id=plane_peer(r), device_id_type=MESH)
    pl.semaphore_signal(barrier, inc=1, device_id=sibling, device_id_type=MESH)

    load_cid.wait()
    cid = cid_ref[...]
    cx, cz, cy = cid >> 5, (cid >> 2) & 7, cid & 3
    dz = (cz - z) & 7
    step = jnp.where(dz <= 4, 2 * dz - 1, 2 * (ZS - dz))
    step = jnp.where(dz == 0, 0, step)
    across = ((cx - x) & 3) * YS + ((cy - y) & 3)
    hot = lax.broadcasted_iota(i32, (ZS * PLANE, rows), 0) == step * PLANE + across
    hot_f = jnp.where(hot, 1.0, 0.0)
    onehot[...] = hot_f.astype(bf16)
    upper = lax.broadcasted_iota(i32, (rows, rows), 0) < lax.broadcasted_iota(i32, (rows, rows), 1)
    before = jnp.dot(onehot[...], jnp.where(upper, 1.0, 0.0).astype(bf16), preferred_element_type=f32)
    place = jnp.sum(hot_f * before, axis=0, keepdims=True).astype(i32)
    lane = across * CAP + place
    slot = step * BLOCK + lane
    at_lane = lax.broadcasted_iota(i32, (128, rows), 0) == lane

    load.wait()
    wide = emb[...].astype(f32)
    scale = lax.rsqrt(jnp.sum(wide * wide, axis=1, keepdims=True) + 1e-06)
    normed[...] = (wide * scale).astype(bf16)

    def place_rows(first, count):
        span = count * BLOCK
        ids = lax.broadcasted_iota(i32, (span, rows), 0) + first * BLOCK
        pick = jnp.where(ids == slot, 1.0, 0.0).astype(bf16)
        placed = jnp.dot(pick, normed[...], preferred_element_type=f32)
        placed = placed.reshape(count * PLANE, CAP, width)
        paired = jnp.concatenate([placed[:, :, :half], placed[:, :, half:]], axis=1)
        snd[first : first + count] = paired.astype(bf16).reshape(count, PLANE, 2 * CAP, half)

    def source(j):
        return snd if j == 0 else zrcv

    def send_z(u):
        j, lo, hi = UNITS[u]
        some = pl.ds(lo, hi - lo)
        src = early.at[j - EARLY, some] if j >= EARLY else snd.at[j, some]
        send(src, zrcv.at[j, some], z_send, z_recv.at[u], z_peer(Z_OFFSETS[j]))

    def send_early(j):
        early[j - EARLY, 0] = snd[j, 0]
        for r in range(1, PLANE):
            send(snd.at[j, r], early.at[j - EARLY, r], e_send, e_recv.at[j - EARLY], plane_peer(r))

    def early_here(j):
        wait_for(early.at[j - EARLY, pl.ds(1, PLANE - 1)], e_recv.at[j - EARLY])

    def send_plane(u):
        j, lo, hi = UNITS[u]
        for r in range(max(lo, 1), hi):
            send(source(j).at[j, r], prcv.at[j, r], p_send, p_recv.at[u], plane_peer(r))

    def rank_along():
        load_rank.wait()
        number = rank_ref[...] + 1
        table = jnp.zeros((ZS * PLANE, 128), f32)
        for shift in (0, 6, 12):
            digit = ((number >> shift) & 63).astype(f32)
            spread = jnp.where(at_lane, digit, 0.0).astype(bf16)
            table += contract_last(onehot[...], spread) * float(1 << shift)
        rsnd[...] = table.reshape(ZS, PLANE, 128)
        for j in range(1, ZS):
            send(rsnd.at[j], zrk.at[j], r1_send, r1_recv, z_peer(Z_OFFSETS[j]))

    def rank_within():
        wait_for(zrk.at[pl.ds(1, ZS - 1)], r1_recv)
        steps = [rsnd[0]] + [zrk[j] for j in range(1, ZS)]
        for r in range(PLANE):
            rmid[r] = jnp.concatenate([step_rank[r : r + 1] for step_rank in steps], axis=0)
        for r in range(1, PLANE):
            send(rmid.at[r], prk.at[r], r2_send, r2_recv, plane_peer(r))

    def spread_ranks(ranks, base):
        for j in range(ZS):
            key_rank[base + j] = jnp.transpose(jnp.broadcast_to(ranks[j], (BLOCK, BLOCK)))

    def rank_done():
        wait_for(prk.at[pl.ds(1, PLANE - 1)], r2_recv)
        found = rmid[0] + jnp.sum(prk[1:], axis=0)
        found = jnp.where(found == 0.0, BEYOND, found - 1.0)
        for j in range(ZS):
            rown[j] = found[j : j + 1]
        send(rown, rsib, r3_send, r3_recv, sibling)
        spread_ranks(rown, 0)

    def rank_sibling():
        wait_for(rsib, r3_recv)
        spread_ranks(rsib, ZS)

    def hand_over(u):
        j, lo, hi = UNITS[u]
        if j >= EARLY:
            wait_for(zrcv.at[j, pl.ds(lo, hi - lo)], z_recv.at[u])
            block = zrcv[j, lo:hi]
        else:
            wait_for(prcv.at[j, pl.ds(1, PLANE - 1)], p_recv.at[j])
            block = jnp.concatenate([source(j)[j, 0:1], prcv[j, 1:]], axis=0)
        block = block.astype(f32)
        size = (hi - lo) * CAP
        low = block[:, :CAP, :].reshape(size, half)
        high = block[:, CAP:, :].reshape(size, half)
        own[j, lo * CAP : hi * CAP] = jnp.concatenate([low, high], axis=1).astype(bf16)
        some = pl.ds(lo * CAP, size)
        send(own.at[j, some], sib.at[j, some], s_send, s_recv.at[u], sibling)

    def score(keys, ranks, queries):
        first, count = queries
        wanted = own[first : first + count].reshape(count * BLOCK, width)
        scores = contract_last(keys, wanted)
        for i in range(count):
            part = scores[:, i * BLOCK : (i + 1) * BLOCK]
            part = jnp.where(ranks < rown[first + i], part, -1.0)
            best = jnp.max(part.reshape(-1, 8, BLOCK), axis=0)
            acc[first + i] = jnp.maximum(acc[first + i], best)

    def keys_of(j, lo, hi):
        span = slice(lo * CAP, hi * CAP)
        keys = jnp.concatenate([own[j, span], sib[j, span]], axis=0)
        ranks = jnp.concatenate([key_rank[j, span], key_rank[ZS + j, span]], axis=0)
        return keys, ranks

    def scores_of(u):
        j, lo, hi = UNITS[u]
        some = sib.at[j, pl.ds(lo * CAP, (hi - lo) * CAP)]
        wait_for(some, s_recv.at[u])
        keys, ranks = keys_of(j, lo, hi)
        last = j + 1 if hi - lo == PLANE else j
        for i in range(0, last, 2):
            score(keys, ranks, (i, min(2, last - i)))
        if hi == PLANE:
            for k in range(j + 1 if last == j else j):
                score(*keys_of(k, 0, PLANE), (j, 1))

    place_rows(1, 2)
    pl.semaphore_wait(barrier, ZS - 1 + PLANE - 1 + 1)
    send_z(1)
    send_z(2)
    place_rows(5, 2)
    send_early(5)
    send_early(6)
    rank_along()
    place_rows(3, 2)
    send_z(3)
    send_z(4)
    place_rows(7, 1)
    send_early(7)
    place_rows(0, 1)
    send_plane(0)
    acc[...] = jnp.full(acc.shape, -1.0, f32)

    def pass_on(u):
        wait_for(zrcv.at[u], z_recv.at[u])
        send_plane(u)

    early_here(5)
    send_z(5)
    early_here(6)
    send_z(6)
    pass_on(1)
    pass_on(2)
    early_here(7)
    send_z(7)
    send_z(8)
    rank_within()
    for u in range(3):
        hand_over(u)
    rank_done()
    pass_on(3)
    pass_on(4)
    rank_sibling()
    for u in range(3):
        scores_of(u)
    hand_over(3)
    hand_over(4)
    scores_of(3)
    scores_of(4)
    hand_over(5)
    hand_over(6)
    scores_of(5)
    scores_of(6)
    hand_over(7)
    hand_over(8)
    scores_of(7)
    scores_of(8)

    for j in range(ZS):
        res[j] = jnp.max(acc[j], axis=0, keepdims=True)
    for j in range(1, ZS):
        send(res.at[j], zres.at[j], o1_send, o1_recv, z_peer(ZS - Z_OFFSETS[j]))
    wait_for(zres.at[pl.ds(1, ZS - 1)], o1_recv)
    zmid[...] = jnp.concatenate([res[0]] + [zres[j] for j in range(1, ZS)], axis=0)
    for r in range(1, PLANE):
        send(zmid, fin.at[r], o2_send, o2_recv, plane_back(r))
    at_step = lax.broadcasted_iota(i32, (ZS, rows), 0) == step
    place_of = jnp.where(at_lane, 1.0, 0.0).astype(bf16)
    wait_for(fin.at[pl.ds(1, PLANE - 1)], o2_recv)
    group = lax.broadcasted_iota(i32, (ZS, 128), 1) // CAP
    back = jnp.where(group == 0, zmid[...], 0.0)
    for r in range(1, PLANE):
        back = jnp.where(group == r, fin[r], back)
    total = jnp.zeros((ZS, rows), f32)
    for _ in range(3):
        part = back.astype(bf16)
        total += jnp.dot(part, place_of, preferred_element_type=f32)
        back = back - part.astype(f32)
    out_ref[...] = jnp.sum(jnp.where(at_step, total, 0.0), axis=0, keepdims=True)

    wait_for(snd.at[pl.ds(1, ZS - 1)], z_send)
    wait_for(prcv.at[:, pl.ds(1, PLANE - 1)], p_send)
    wait_for(early.at[:, pl.ds(1, PLANE - 1)], e_send)
    wait_for(own, s_send)
    wait_for(zrk.at[pl.ds(1, ZS - 1)], r1_send)
    wait_for(prk.at[pl.ds(1, PLANE - 1)], r2_send)
    wait_for(rown, r3_send)
    wait_for(zres.at[pl.ds(1, ZS - 1)], o1_send)
    wait_for(fin.at[pl.ds(1, PLANE - 1)], o2_send)


def body(embeddings, cluster_id, rank):
    rows, width = embeddings.shape
    half = width // 2
    blocks = (ZS, PLANE, 2 * CAP, half)
    vmem = pltpu.VMEM
    dma = pltpu.SemaphoreType.DMA
    out = pl.pallas_call(
        kernel,
        out_shape=jax.ShapeDtypeStruct((1, rows), f32),
        in_specs=[pl.BlockSpec(memory_space=pltpu.HBM)] * 3,
        out_specs=pl.BlockSpec(memory_space=vmem),
        scratch_shapes=[
            vmem((rows, width), bf16),
            vmem((1, rows), i32),
            vmem((1, rows), i32),
            vmem((rows, width), bf16),
            vmem((ZS * PLANE, rows), bf16),
            vmem(blocks, bf16),
            vmem((ZS - EARLY,) + blocks[1:], bf16),
            vmem(blocks, bf16),
            vmem((EARLY,) + blocks[1:], bf16),
            vmem((ZS, BLOCK, width), bf16),
            vmem((ZS, BLOCK, width), bf16),
            vmem((ZS, PLANE, 128), f32),
            vmem((ZS, PLANE, 128), f32),
            vmem((PLANE, ZS, 128), f32),
            vmem((PLANE, ZS, 128), f32),
            vmem((ZS, 1, 128), f32),
            vmem((ZS, 1, 128), f32),
            vmem((2 * ZS, BLOCK, BLOCK), f32),
            vmem((ZS, 8, BLOCK), f32),
            vmem((ZS, 1, 128), f32),
            vmem((ZS, 1, 128), f32),
            vmem((ZS, 128), f32),
            vmem((PLANE, ZS, 128), f32),
            dma, dma, dma, dma, dma((len(UNITS),)), dma, dma((EARLY,)), dma, dma((ZS - EARLY,)), dma, dma((len(UNITS),)),
            dma, dma, dma, dma, dma, dma, dma, dma, dma, dma,
        ],
        compiler_params=pltpu.CompilerParams(
            collective_id=0, has_side_effects=True, vmem_limit_bytes=62 << 20
        ),
        name="exchange_and_score",
    )(embeddings, cluster_id.reshape(1, rows), rank.reshape(1, rows))
    return out.reshape(rows)


def solution(mesh):
    in_specs = (P(("ingest", "span"), None), P(("ingest", "span")), P(("ingest", "span")))
    out_specs = P(("ingest", "span"))
    return jax.shard_map(body, mesh=mesh, in_specs=in_specs, out_specs=out_specs, check_vma=False)
```

```python
import jax
import jax.numpy as jnp
from jax import lax
from jax.experimental import pallas as pl
from jax.experimental.pallas import tpu as pltpu
from jax.sharding import PartitionSpec as P

XS, ZS, YS = 4, 8, 4
PLANE = XS * YS
CAP = 8
BLOCK = PLANE * CAP
BEYOND = float(2**30)
MESH = pl.DeviceIdType.MESH
Z_OFFSETS = (0, 1, 7, 2, 6, 3, 5, 4)
LAST = ZS - 1
EARLY = 5
UNITS = tuple((j, 0, PLANE) for j in range(ZS - 1)) + ((ZS - 1, 0, PLANE // 2), (ZS - 1, PLANE // 2, PLANE))


def distance(step, r):
    dx, dz, dy = r // YS, Z_OFFSETS[step], r % YS
    return min(dx, XS - dx) + min(dz, ZS - dz) + min(dy, YS - dy)


RETURNS = sorted(
    ((j, r) for j in range(ZS) for r in range(PLANE) if (j, r) != (0, 0)), key=lambda jr: -distance(*jr)
)
f32, bf16, i32 = jnp.float32, jnp.bfloat16, jnp.int32


def contract_last(a, b):
    return lax.dot_general(a, b, (((1,), (1,)), ((), ())), preferred_element_type=f32)


def kernel(
    emb_hbm, cid_hbm, rank_hbm, out_ref,
    emb, cid_ref, rank_ref, normed, onehot, snd, early, zrcv, prcv, own, sib,
    rsnd, zrk, rmid, prk, rown, rsib, key_rank, acc, res, fin,
    emb_sem, cid_sem, rank_sem, z_send, z_recv, p_send, p_recv, e_send, e_recv, s_send, s_recv,
    r1_send, r1_recv, r2_send, r2_recv, r3_send, r3_recv, o_send, o_recv,
):
    rows = cid_ref.shape[1]
    width = emb.shape[1]
    half = width // 2
    me = lax.axis_index("ingest")
    core = lax.axis_index("span")
    x, z, y = me // (ZS * YS), (me // YS) % ZS, me % YS

    def chip(px, pz, py):
        return (px * ZS + pz) * YS + py

    def z_peer(offset):
        return (chip(x, lax.rem(z + offset, ZS), y), core)

    def plane_peer(r):
        return (chip(lax.rem(x + r // YS, XS), z, lax.rem(y + r % YS, YS)), core)

    def plane_back(r):
        return (chip(lax.rem(x + XS - r // YS, XS), z, lax.rem(y + YS - r % YS, YS)), core)

    sibling = (me, 1 - core)

    def send(src, dst, send_sem, recv_sem, device):
        pltpu.make_async_remote_copy(
            src_ref=src, dst_ref=dst, send_sem=send_sem, recv_sem=recv_sem,
            device_id=device, device_id_type=MESH,
        ).start()

    def wait_for(ref, sem):
        pltpu.make_async_copy(ref, ref, sem).wait()

    load_cid = pltpu.make_async_copy(cid_hbm, cid_ref, cid_sem)
    load_cid.start()
    load = pltpu.make_async_copy(emb_hbm, emb, emb_sem)
    load.start()
    load_rank = pltpu.make_async_copy(rank_hbm, rank_ref, rank_sem)
    load_rank.start()
    barrier = pltpu.get_barrier_semaphore()
    for offset in range(1, ZS):
        pl.semaphore_signal(barrier, inc=1, device_id=z_peer(offset), device_id_type=MESH)
    for r in range(1, PLANE):
        pl.semaphore_signal(barrier, inc=1, device_id=plane_peer(r), device_id_type=MESH)
    pl.semaphore_signal(barrier, inc=1, device_id=sibling, device_id_type=MESH)

    load_cid.wait()
    cid = cid_ref[...]
    cx, cz, cy = cid >> 5, (cid >> 2) & 7, cid & 3
    dz = (cz - z) & 7
    step = jnp.where(dz <= 4, 2 * dz - 1, 2 * (ZS - dz))
    step = jnp.where(dz == 0, 0, step)
    across = ((cx - x) & 3) * YS + ((cy - y) & 3)
    hot = lax.broadcasted_iota(i32, (ZS * PLANE, rows), 0) == step * PLANE + across
    hot_f = jnp.where(hot, 1.0, 0.0)
    onehot[...] = hot_f.astype(bf16)
    upper = lax.broadcasted_iota(i32, (rows, rows), 0) < lax.broadcasted_iota(i32, (rows, rows), 1)
    before = jnp.dot(onehot[...], jnp.where(upper, 1.0, 0.0).astype(bf16), preferred_element_type=f32)
    place = jnp.sum(hot_f * before, axis=0, keepdims=True).astype(i32)
    lane = across * CAP + place
    slot = step * BLOCK + lane
    at_lane = lax.broadcasted_iota(i32, (128, rows), 0) == lane

    load.wait()
    wide = emb[...].astype(f32)
    scale = lax.rsqrt(jnp.sum(wide * wide, axis=1, keepdims=True) + 1e-06)
    normed[...] = (wide * scale).astype(bf16)

    def place_rows(first, count):
        span = count * BLOCK
        ids = lax.broadcasted_iota(i32, (span, rows), 0) + first * BLOCK
        pick = jnp.where(ids == slot, 1.0, 0.0).astype(bf16)
        placed = jnp.dot(pick, normed[...], preferred_element_type=f32)
        placed = placed.reshape(count * PLANE, CAP, width)
        paired = jnp.concatenate([placed[:, :, :half], placed[:, :, half:]], axis=1)
        snd[first : first + count] = paired.astype(bf16).reshape(count, PLANE, 2 * CAP, half)

    def source(j):
        return snd if j == 0 else zrcv

    def send_z(u):
        j, lo, hi = UNITS[u]
        some = pl.ds(lo, hi - lo)
        src = early.at[j - EARLY, some] if j >= EARLY else snd.at[j, some]
        send(src, zrcv.at[j, some], z_send, z_recv.at[u], z_peer(Z_OFFSETS[j]))

    def send_early(j):
        early[j - EARLY, 0] = snd[j, 0]
        for r in range(1, PLANE):
            send(snd.at[j, r], early.at[j - EARLY, r], e_send, e_recv.at[j - EARLY], plane_peer(r))

    def early_here(j):
        wait_for(early.at[j - EARLY, pl.ds(1, PLANE - 1)], e_recv.at[j - EARLY])

    def send_plane(u):
        j, lo, hi = UNITS[u]
        for r in range(max(lo, 1), hi):
            send(source(j).at[j, r], prcv.at[j, r], p_send, p_recv.at[u], plane_peer(r))

    def rank_along():
        load_rank.wait()
        number = rank_ref[...] + 1
        table = jnp.zeros((ZS * PLANE, 128), f32)
        for shift in (0, 6, 12):
            digit = ((number >> shift) & 63).astype(f32)
            spread = jnp.where(at_lane, digit, 0.0).astype(bf16)
            table += contract_last(onehot[...], spread) * float(1 << shift)
        rsnd[...] = table.reshape(ZS, PLANE, 128)
        for j in range(1, ZS):
            send(rsnd.at[j], zrk.at[j], r1_send, r1_recv, z_peer(Z_OFFSETS[j]))

    def rank_within():
        wait_for(zrk.at[pl.ds(1, ZS - 1)], r1_recv)
        steps = [rsnd[0]] + [zrk[j] for j in range(1, ZS)]
        for r in range(PLANE):
            rmid[r] = jnp.concatenate([step_rank[r : r + 1] for step_rank in steps], axis=0)
        for r in range(1, PLANE):
            send(rmid.at[r], prk.at[r], r2_send, r2_recv, plane_peer(r))

    def spread_ranks(ranks, base):
        for j in range(ZS):
            key_rank[base + j] = jnp.transpose(jnp.broadcast_to(ranks[j], (BLOCK, BLOCK)))

    def rank_done():
        wait_for(prk.at[pl.ds(1, PLANE - 1)], r2_recv)
        found = rmid[0] + jnp.sum(prk[1:], axis=0)
        found = jnp.where(found == 0.0, BEYOND, found - 1.0)
        for j in range(ZS):
            rown[j] = found[j : j + 1]
        send(rown, rsib, r3_send, r3_recv, sibling)
        spread_ranks(rown, 0)

    def rank_sibling():
        wait_for(rsib, r3_recv)
        spread_ranks(rsib, ZS)

    def hand_over(u):
        j, lo, hi = UNITS[u]
        if j >= EARLY:
            wait_for(zrcv.at[j, pl.ds(lo, hi - lo)], z_recv.at[u])
            block = zrcv[j, lo:hi]
        else:
            wait_for(prcv.at[j, pl.ds(1, PLANE - 1)], p_recv.at[j])
            block = jnp.concatenate([source(j)[j, 0:1], prcv[j, 1:]], axis=0)
        block = block.astype(f32)
        size = (hi - lo) * CAP
        low = block[:, :CAP, :].reshape(size, half)
        high = block[:, CAP:, :].reshape(size, half)
        own[j, lo * CAP : hi * CAP] = jnp.concatenate([low, high], axis=1).astype(bf16)
        some = pl.ds(lo * CAP, size)
        send(own.at[j, some], sib.at[j, some], s_send, s_recv.at[u], sibling)

    def score(keys, ranks, queries):
        first, count = queries
        wanted = own[first : first + count].reshape(count * BLOCK, width)
        scores = contract_last(keys, wanted)
        for i in range(count):
            part = scores[:, i * BLOCK : (i + 1) * BLOCK]
            part = jnp.where(ranks < rown[first + i], part, -1.0)
            best = jnp.max(part.reshape(-1, 8, BLOCK), axis=0)
            acc[first + i] = jnp.maximum(acc[first + i], best)

    def keys_of(j, lo, hi):
        span = slice(lo * CAP, hi * CAP)
        keys = jnp.concatenate([own[j, span], sib[j, span]], axis=0)
        ranks = jnp.concatenate([key_rank[j, span], key_rank[ZS + j, span]], axis=0)
        return keys, ranks

    def scores_of(u):
        j, lo, hi = UNITS[u]
        some = sib.at[j, pl.ds(lo * CAP, (hi - lo) * CAP)]
        wait_for(some, s_recv.at[u])
        keys, ranks = keys_of(j, lo, hi)
        last = j + 1 if hi - lo == PLANE else j
        for i in range(0, last, 2):
            score(keys, ranks, (i, min(2, last - i)))
        if hi == PLANE:
            for k in range(j + 1 if last == j else j):
                score(*keys_of(k, 0, PLANE), (j, 1))

    place_rows(1, 2)
    pl.semaphore_wait(barrier, ZS - 1 + PLANE - 1 + 1)
    send_z(1)
    send_z(2)
    place_rows(5, 2)
    send_early(5)
    send_early(6)
    rank_along()
    place_rows(3, 2)
    send_z(3)
    send_z(4)
    place_rows(7, 1)
    send_early(7)
    place_rows(0, 1)
    send_plane(0)
    acc[...] = jnp.full(acc.shape, -1.0, f32)

    def pass_on(u):
        wait_for(zrcv.at[u], z_recv.at[u])
        send_plane(u)

    early_here(5)
    send_z(5)
    early_here(6)
    send_z(6)
    pass_on(1)
    pass_on(2)
    early_here(7)
    send_z(7)
    send_z(8)
    rank_within()
    for u in range(3):
        hand_over(u)
    rank_done()
    pass_on(3)
    pass_on(4)
    rank_sibling()
    for u in range(3):
        scores_of(u)
    hand_over(3)
    hand_over(4)
    scores_of(3)
    scores_of(4)
    hand_over(5)
    hand_over(6)
    scores_of(5)
    scores_of(6)
    hand_over(7)
    hand_over(8)
    scores_of(7)
    scores_of(8)

    for j in range(ZS):
        res[j] = jnp.max(acc[j], axis=0, keepdims=True)
    for j, r in RETURNS:
        px, pz = lax.rem(x + XS - r // YS, XS), lax.rem(z + ZS - Z_OFFSETS[j], ZS)
        device = (chip(px, pz, lax.rem(y + YS - r % YS, YS)), core)
        send(res.at[j], fin.at[j * PLANE + r], o_send, o_recv, device)
    fin[0] = res[0]
    at_step = lax.broadcasted_iota(i32, (ZS, rows), 0) == step
    place_of = jnp.where(at_lane, 1.0, 0.0).astype(bf16)
    group = lax.broadcasted_iota(i32, (1, 128), 1) // CAP
    wait_for(fin.at[pl.ds(1, ZS * PLANE - 1)], o_recv)
    lines = []
    for j in range(ZS):
        line = jnp.zeros((1, 128), f32)
        for r in range(PLANE):
            line = jnp.where(group == r, fin[j * PLANE + r], line)
        lines.append(line)
    back = jnp.concatenate(lines, axis=0)
    parts = []
    for _ in range(3):
        parts.append(back.astype(bf16))
        back = back - parts[-1].astype(f32)
    parts = jnp.dot(jnp.concatenate(parts, axis=0), place_of, preferred_element_type=f32)
    total = parts[:ZS] + parts[ZS : 2 * ZS] + parts[2 * ZS :]
    out_ref[...] = jnp.sum(jnp.where(at_step, total, 0.0), axis=0, keepdims=True)

    wait_for(snd.at[pl.ds(1, ZS - 1)], z_send)
    wait_for(prcv.at[:, pl.ds(1, PLANE - 1)], p_send)
    wait_for(early.at[:, pl.ds(1, PLANE - 1)], e_send)
    wait_for(own, s_send)
    wait_for(zrk.at[pl.ds(1, ZS - 1)], r1_send)
    wait_for(prk.at[pl.ds(1, PLANE - 1)], r2_send)
    wait_for(rown, r3_send)
    wait_for(fin.at[pl.ds(1, ZS * PLANE - 1)], o_send)


def body(embeddings, cluster_id, rank):
    rows, width = embeddings.shape
    half = width // 2
    blocks = (ZS, PLANE, 2 * CAP, half)
    vmem = pltpu.VMEM
    dma = pltpu.SemaphoreType.DMA
    out = pl.pallas_call(
        kernel,
        out_shape=jax.ShapeDtypeStruct((1, rows), f32),
        in_specs=[pl.BlockSpec(memory_space=pltpu.HBM)] * 3,
        out_specs=pl.BlockSpec(memory_space=vmem),
        scratch_shapes=[
            vmem((rows, width), bf16),
            vmem((1, rows), i32),
            vmem((1, rows), i32),
            vmem((rows, width), bf16),
            vmem((ZS * PLANE, rows), bf16),
            vmem(blocks, bf16),
            vmem((ZS - EARLY,) + blocks[1:], bf16),
            vmem(blocks, bf16),
            vmem((EARLY,) + blocks[1:], bf16),
            vmem((ZS, BLOCK, width), bf16),
            vmem((ZS, BLOCK, width), bf16),
            vmem((ZS, PLANE, 128), f32),
            vmem((ZS, PLANE, 128), f32),
            vmem((PLANE, ZS, 128), f32),
            vmem((PLANE, ZS, 128), f32),
            vmem((ZS, 1, 128), f32),
            vmem((ZS, 1, 128), f32),
            vmem((2 * ZS, BLOCK, BLOCK), f32),
            vmem((ZS, 8, BLOCK), f32),
            vmem((ZS, 1, 128), f32),
            vmem((ZS * PLANE, 1, 128), f32),
            dma, dma, dma, dma, dma((len(UNITS),)), dma, dma((EARLY,)), dma, dma((ZS - EARLY,)), dma, dma((len(UNITS),)),
            dma, dma, dma, dma, dma, dma, dma, dma,
        ],
        compiler_params=pltpu.CompilerParams(
            collective_id=0, has_side_effects=True, vmem_limit_bytes=62 << 20
        ),
        name="exchange_and_score",
    )(embeddings, cluster_id.reshape(1, rows), rank.reshape(1, rows))
    return out.reshape(rows)


def solution(mesh):
    in_specs = (P(("ingest", "span"), None), P(("ingest", "span")), P(("ingest", "span")))
    out_specs = P(("ingest", "span"))
    return jax.shard_map(body, mesh=mesh, in_specs=in_specs, out_specs=out_specs, check_vma=False)
```

```python
import jax
import jax.numpy as jnp
from jax import lax
from jax.experimental import pallas as pl
from jax.experimental.pallas import tpu as pltpu
from jax.sharding import PartitionSpec as P

XS, ZS, YS = 4, 8, 4
PLANE = XS * YS
CAP = 8
BLOCK = PLANE * CAP
BEYOND = float(2**30)
MESH = pl.DeviceIdType.MESH
Z_OFFSETS = (0, 1, 7, 2, 6, 3, 5, 4)
LAST = ZS - 1
EARLY = 5
UNITS = tuple((j, 0, PLANE) for j in range(ZS - 1)) + ((ZS - 1, 0, PLANE // 2), (ZS - 1, PLANE // 2, PLANE))


def distance(step, r):
    dx, dz, dy = r // YS, Z_OFFSETS[step], r % YS
    return min(dx, XS - dx) + min(dz, ZS - dz) + min(dy, YS - dy)


RETURNS = sorted(
    ((j, r) for j in range(ZS) for r in range(PLANE) if (j, r) != (0, 0)), key=lambda jr: -distance(*jr)
)
f32, bf16, i32 = jnp.float32, jnp.bfloat16, jnp.int32


def contract_last(a, b):
    return lax.dot_general(a, b, (((1,), (1,)), ((), ())), preferred_element_type=f32)


def kernel(
    emb_hbm, cid_hbm, rank_hbm, out_ref,
    emb, cid_ref, rank_ref, normed, onehot, snd, early, zrcv, prcv, own, sib,
    rsnd, zrk, rmid, prk, rown, rsib, key_rank, acc, res, fin,
    emb_sem, cid_sem, rank_sem, z_send, z_recv, p_send, p_recv, e_send, e_recv, s_send, s_recv,
    r1_send, r1_recv, r2_send, r2_recv, r3_send, r3_recv, o_send, o_recv,
):
    rows = cid_ref.shape[1]
    width = emb.shape[1]
    half = width // 2
    me = lax.axis_index("ingest")
    core = lax.axis_index("span")
    x, z, y = me // (ZS * YS), (me // YS) % ZS, me % YS

    def chip(px, pz, py):
        return (px * ZS + pz) * YS + py

    xs = [lax.rem(x + d, XS) for d in range(XS)]
    zs = [lax.rem(z + d, ZS) for d in range(ZS)]
    ys = [lax.rem(y + d, YS) for d in range(YS)]

    def z_peer(offset):
        return (chip(x, zs[offset], y), core)

    def plane_peer(r):
        return (chip(xs[r // YS], z, ys[r % YS]), core)

    def origin(j, r):
        return (chip(xs[-(r // YS) % XS], zs[-Z_OFFSETS[j] % ZS], ys[-(r % YS) % YS]), core)

    sibling = (me, 1 - core)

    def send(src, dst, send_sem, recv_sem, device):
        pltpu.make_async_remote_copy(
            src_ref=src, dst_ref=dst, send_sem=send_sem, recv_sem=recv_sem,
            device_id=device, device_id_type=MESH,
        ).start()

    def wait_for(ref, sem):
        pltpu.make_async_copy(ref, ref, sem).wait()

    load_cid = pltpu.make_async_copy(cid_hbm, cid_ref, cid_sem)
    load_cid.start()
    load = pltpu.make_async_copy(emb_hbm, emb, emb_sem)
    load.start()
    load_rank = pltpu.make_async_copy(rank_hbm, rank_ref, rank_sem)
    load_rank.start()
    barrier = pltpu.get_barrier_semaphore()
    for offset in range(1, ZS):
        pl.semaphore_signal(barrier, inc=1, device_id=z_peer(offset), device_id_type=MESH)
    for r in range(1, PLANE):
        pl.semaphore_signal(barrier, inc=1, device_id=plane_peer(r), device_id_type=MESH)
    pl.semaphore_signal(barrier, inc=1, device_id=sibling, device_id_type=MESH)

    load_cid.wait()
    cid = cid_ref[...]
    cx, cz, cy = cid >> 5, (cid >> 2) & 7, cid & 3
    dz = (cz - z) & 7
    step = jnp.where(dz <= 4, 2 * dz - 1, 2 * (ZS - dz))
    step = jnp.where(dz == 0, 0, step)
    across = ((cx - x) & 3) * YS + ((cy - y) & 3)
    hot = lax.broadcasted_iota(i32, (ZS * PLANE, rows), 0) == step * PLANE + across
    hot_f = jnp.where(hot, 1.0, 0.0)
    onehot[...] = hot_f.astype(bf16)
    upper = lax.broadcasted_iota(i32, (rows, rows), 0) < lax.broadcasted_iota(i32, (rows, rows), 1)
    before = jnp.dot(onehot[...], jnp.where(upper, 1.0, 0.0).astype(bf16), preferred_element_type=f32)
    place = jnp.sum(hot_f * before, axis=0, keepdims=True).astype(i32)
    lane = across * CAP + place
    slot = step * BLOCK + lane
    at_lane = lax.broadcasted_iota(i32, (128, rows), 0) == lane
    at_step = lax.broadcasted_iota(i32, (ZS, rows), 0) == step
    step_hot = jnp.where(at_step, 1.0, 0.0).astype(bf16)
    group = lax.broadcasted_iota(i32, (1, 128), 1) // CAP

    load.wait()
    wide = emb[...].astype(f32)
    scale = lax.rsqrt(jnp.sum(wide * wide, axis=1, keepdims=True) + 1e-06)
    normed[...] = (wide * scale).astype(bf16)

    def place_rows(first, count):
        span = count * BLOCK
        ids = lax.broadcasted_iota(i32, (span, rows), 0) + first * BLOCK
        pick = jnp.where(ids == slot, 1.0, 0.0).astype(bf16)
        placed = jnp.dot(pick, normed[...], preferred_element_type=f32)
        placed = placed.reshape(count * PLANE, CAP, width)
        paired = jnp.concatenate([placed[:, :, :half], placed[:, :, half:]], axis=1)
        snd[first : first + count] = paired.astype(bf16).reshape(count, PLANE, 2 * CAP, half)

    def source(j):
        return snd if j == 0 else zrcv

    def send_z(u):
        j, lo, hi = UNITS[u]
        some = pl.ds(lo, hi - lo)
        src = early.at[j - EARLY, some] if j >= EARLY else snd.at[j, some]
        send(src, zrcv.at[j, some], z_send, z_recv.at[u], z_peer(Z_OFFSETS[j]))

    def send_early(j):
        early[j - EARLY, 0] = snd[j, 0]
        for r in range(1, PLANE):
            send(snd.at[j, r], early.at[j - EARLY, r], e_send, e_recv.at[j - EARLY], plane_peer(r))

    def early_here(j):
        wait_for(early.at[j - EARLY, pl.ds(1, PLANE - 1)], e_recv.at[j - EARLY])

    def send_plane(u):
        j, lo, hi = UNITS[u]
        for r in range(max(lo, 1), hi):
            send(source(j).at[j, r], prcv.at[j, r], p_send, p_recv.at[u], plane_peer(r))

    def rank_along():
        load_rank.wait()
        number = rank_ref[...] + 1
        table = jnp.zeros((ZS, 128), f32)
        for shift in (0, 6, 12):
            digit = ((number >> shift) & 63).astype(f32)
            spread = jnp.where(at_lane, digit, 0.0).astype(bf16)
            table += contract_last(step_hot, spread) * float(1 << shift)
        for j in range(ZS):
            rsnd[j] = table[j : j + 1]
        for j in range(1, ZS):
            send(rsnd.at[j], zrk.at[j], r1_send, r1_recv, z_peer(Z_OFFSETS[j]))

    def rank_within():
        wait_for(zrk.at[pl.ds(1, ZS - 1)], r1_recv)
        rmid[...] = jnp.concatenate([rsnd[0]] + [zrk[j] for j in range(1, ZS)], axis=0)
        for r in range(1, PLANE):
            send(rmid, prk.at[r], r2_send, r2_recv, plane_peer(r))

    def spread_ranks(ranks, base):
        for j in range(ZS):
            key_rank[base + j] = jnp.transpose(jnp.broadcast_to(ranks[j], (BLOCK, BLOCK)))

    def rank_done():
        wait_for(prk.at[pl.ds(1, PLANE - 1)], r2_recv)
        found = rmid[...]
        for r in range(1, PLANE):
            found = jnp.where(group == r, prk[r], found)
        found = jnp.where(found == 0.0, BEYOND, found - 1.0)
        for j in range(ZS):
            rown[j] = found[j : j + 1]
        send(rown, rsib, r3_send, r3_recv, sibling)
        spread_ranks(rown, 0)

    def rank_sibling():
        wait_for(rsib, r3_recv)
        spread_ranks(rsib, ZS)

    def hand_over(u):
        j, lo, hi = UNITS[u]
        if j >= EARLY:
            wait_for(zrcv.at[j, pl.ds(lo, hi - lo)], z_recv.at[u])
            block = zrcv[j, lo:hi]
        else:
            wait_for(prcv.at[j, pl.ds(1, PLANE - 1)], p_recv.at[j])
            block = jnp.concatenate([source(j)[j, 0:1], prcv[j, 1:]], axis=0)
        block = block.astype(f32)
        size = (hi - lo) * CAP
        low = block[:, :CAP, :].reshape(size, half)
        high = block[:, CAP:, :].reshape(size, half)
        own[j, lo * CAP : hi * CAP] = jnp.concatenate([low, high], axis=1).astype(bf16)
        some = pl.ds(lo * CAP, size)
        send(own.at[j, some], sib.at[j, some], s_send, s_recv.at[u], sibling)

    def score(keys, ranks, queries):
        first, count = queries
        wanted = own[first : first + count].reshape(count * BLOCK, width)
        scores = contract_last(keys, wanted)
        for i in range(count):
            part = scores[:, i * BLOCK : (i + 1) * BLOCK]
            part = jnp.where(ranks < rown[first + i], part, -1.0)
            best = jnp.max(part.reshape(-1, 8, BLOCK), axis=0)
            acc[first + i] = jnp.maximum(acc[first + i], best)

    def keys_of(j, lo, hi):
        span = slice(lo * CAP, hi * CAP)
        keys = jnp.concatenate([own[j, span], sib[j, span]], axis=0)
        ranks = jnp.concatenate([key_rank[j, span], key_rank[ZS + j, span]], axis=0)
        return keys, ranks

    def new_keys(u, steps):
        j, lo, hi = UNITS[u]
        wait_for(sib.at[j, pl.ds(lo * CAP, (hi - lo) * CAP)], s_recv.at[u])
        keys, ranks = keys_of(j, lo, hi)
        for i in range(0, steps, 2):
            score(keys, ranks, (i, min(2, steps - i)))

    def new_queries(j):
        for k in range(j):
            score(*keys_of(k, 0, PLANE), (j, 1))

    def scores_of(u):
        new_keys(u, u + 1)
        new_queries(u)

    place_rows(1, 1)
    pl.semaphore_wait(barrier, ZS - 1 + PLANE - 1 + 1)
    send_z(1)
    place_rows(2, 1)
    send_z(2)
    place_rows(5, 2)
    send_early(5)
    send_early(6)
    rank_along()
    place_rows(3, 2)
    send_z(3)
    send_z(4)
    place_rows(7, 1)
    send_early(7)
    place_rows(0, 1)
    send_plane(0)
    acc[...] = jnp.full(acc.shape, -1.0, f32)

    def pass_on(u):
        wait_for(zrcv.at[u], z_recv.at[u])
        send_plane(u)

    early_here(5)
    send_z(5)
    early_here(6)
    send_z(6)
    pass_on(1)
    pass_on(2)
    early_here(7)
    send_z(7)
    send_z(8)
    rank_within()
    for u in range(3):
        hand_over(u)
    rank_done()
    pass_on(3)
    pass_on(4)
    rank_sibling()
    for u in range(3):
        scores_of(u)
    hand_over(3)
    hand_over(4)
    scores_of(3)
    scores_of(4)
    hand_over(5)
    hand_over(6)
    scores_of(5)
    scores_of(6)
    hand_over(7)
    hand_over(8)
    new_queries(LAST)
    new_keys(7, ZS)
    new_keys(8, ZS)

    for j in range(ZS):
        res[j] = jnp.max(acc[j], axis=0, keepdims=True)
    for j, r in RETURNS:
        send(res.at[j], fin.at[j * PLANE + r], o_send, o_recv, origin(j, r))
    fin[0] = res[0]
    place_of = jnp.where(at_lane, 1.0, 0.0).astype(bf16)
    wait_for(fin.at[pl.ds(1, ZS * PLANE - 1)], o_recv)
    lines = []
    for j in range(ZS):
        line = jnp.zeros((1, 128), f32)
        for r in range(PLANE):
            line = jnp.where(group == r, fin[j * PLANE + r], line)
        lines.append(line)
    back = jnp.concatenate(lines, axis=0)
    parts = []
    for _ in range(3):
        parts.append(back.astype(bf16))
        back = back - parts[-1].astype(f32)
    parts = jnp.dot(jnp.concatenate(parts, axis=0), place_of, preferred_element_type=f32)
    total = parts[:ZS] + parts[ZS : 2 * ZS] + parts[2 * ZS :]
    out_ref[...] = jnp.sum(jnp.where(at_step, total, 0.0), axis=0, keepdims=True)

    wait_for(snd.at[pl.ds(1, ZS - 1)], z_send)
    wait_for(prcv.at[:, pl.ds(1, PLANE - 1)], p_send)
    wait_for(early.at[:, pl.ds(1, PLANE - 1)], e_send)
    wait_for(own, s_send)
    wait_for(zrk.at[pl.ds(1, ZS - 1)], r1_send)
    wait_for(prk.at[pl.ds(1, PLANE - 1)], r2_send)
    wait_for(rown, r3_send)
    wait_for(fin.at[pl.ds(1, ZS * PLANE - 1)], o_send)


def body(embeddings, cluster_id, rank):
    rows, width = embeddings.shape
    half = width // 2
    blocks = (ZS, PLANE, 2 * CAP, half)
    vmem = pltpu.VMEM
    dma = pltpu.SemaphoreType.DMA
    out = pl.pallas_call(
        kernel,
        out_shape=jax.ShapeDtypeStruct((1, rows), f32),
        in_specs=[pl.BlockSpec(memory_space=pltpu.HBM)] * 3,
        out_specs=pl.BlockSpec(memory_space=vmem),
        scratch_shapes=[
            vmem((rows, width), bf16),
            vmem((1, rows), i32),
            vmem((1, rows), i32),
            vmem((rows, width), bf16),
            vmem((ZS * PLANE, rows), bf16),
            vmem(blocks, bf16),
            vmem((ZS - EARLY,) + blocks[1:], bf16),
            vmem(blocks, bf16),
            vmem((EARLY,) + blocks[1:], bf16),
            vmem((ZS, BLOCK, width), bf16),
            vmem((ZS, BLOCK, width), bf16),
            vmem((ZS, 1, 128), f32),
            vmem((ZS, 1, 128), f32),
            vmem((ZS, 128), f32),
            vmem((PLANE, ZS, 128), f32),
            vmem((ZS, 1, 128), f32),
            vmem((ZS, 1, 128), f32),
            vmem((2 * ZS, BLOCK, BLOCK), f32),
            vmem((ZS, 8, BLOCK), f32),
            vmem((ZS, 1, 128), f32),
            vmem((ZS * PLANE, 1, 128), f32),
            dma, dma, dma, dma, dma((len(UNITS),)), dma, dma((EARLY,)), dma, dma((ZS - EARLY,)), dma, dma((len(UNITS),)),
            dma, dma, dma, dma, dma, dma, dma, dma,
        ],
        compiler_params=pltpu.CompilerParams(
            collective_id=0, has_side_effects=True, vmem_limit_bytes=62 << 20
        ),
        name="exchange_and_score",
    )(embeddings, cluster_id.reshape(1, rows), rank.reshape(1, rows))
    return out.reshape(rows)


def solution(mesh):
    in_specs = (P(("ingest", "span"), None), P(("ingest", "span")), P(("ingest", "span")))
    out_specs = P(("ingest", "span"))
    return jax.shard_map(body, mesh=mesh, in_specs=in_specs, out_specs=out_specs, check_vma=False)
```

```python
import jax
import jax.numpy as jnp
from jax import lax
from jax.experimental import pallas as pl
from jax.experimental.pallas import tpu as pltpu
from jax.sharding import PartitionSpec as P

XS, ZS, YS = 4, 8, 4
PLANE = XS * YS
CAP = 8
BLOCK = PLANE * CAP
BEYOND = float(2**30)
MESH = pl.DeviceIdType.MESH
Z_OFFSETS = (0, 1, 7, 2, 6, 3, 5, 4)
LAST = ZS - 1
EARLY = 5
UNITS = tuple((j, 0, PLANE) for j in range(ZS - 1)) + ((ZS - 1, 0, PLANE // 2), (ZS - 1, PLANE // 2, PLANE))


def distance(step, r):
    dx, dz, dy = r // YS, Z_OFFSETS[step], r % YS
    return min(dx, XS - dx) + min(dz, ZS - dz) + min(dy, YS - dy)


RETURNS = sorted(
    ((j, r) for j in range(ZS) for r in range(PLANE) if (j, r) != (0, 0)), key=lambda jr: -distance(*jr)
)
f32, bf16, i32 = jnp.float32, jnp.bfloat16, jnp.int32


def contract_last(a, b):
    return lax.dot_general(a, b, (((1,), (1,)), ((), ())), preferred_element_type=f32)


def kernel(
    emb_hbm, cid_hbm, rank_hbm, out_ref,
    emb, cid_ref, rank_ref, normed, onehot, snd, early, zrcv, prcv, own, sib,
    rsnd, zrk, rmid, prk, rown, rsib, key_rank, acc, res, fin,
    emb_sem, cid_sem, rank_sem, z_send, z_recv, p_send, p_recv, e_send, e_recv, s_send, s_recv,
    r1_send, r1_recv, r2_send, r2_recv, r3_send, r3_recv, o_send, o_recv,
):
    rows = cid_ref.shape[1]
    width = emb.shape[1]
    half = width // 2
    me = lax.axis_index("ingest")
    core = lax.axis_index("span")
    x, z, y = me // (ZS * YS), (me // YS) % ZS, me % YS

    def chip(px, pz, py):
        return (px * ZS + pz) * YS + py

    xs = [lax.rem(x + d, XS) for d in range(XS)]
    zs = [lax.rem(z + d, ZS) for d in range(ZS)]
    ys = [lax.rem(y + d, YS) for d in range(YS)]

    def z_peer(offset):
        return (chip(x, zs[offset], y), core)

    def plane_peer(r):
        return (chip(xs[r // YS], z, ys[r % YS]), core)

    def origin(j, r):
        return (chip(xs[-(r // YS) % XS], zs[-Z_OFFSETS[j] % ZS], ys[-(r % YS) % YS]), core)

    sibling = (me, 1 - core)

    def send(src, dst, send_sem, recv_sem, device):
        pltpu.make_async_remote_copy(
            src_ref=src, dst_ref=dst, send_sem=send_sem, recv_sem=recv_sem,
            device_id=device, device_id_type=MESH,
        ).start()

    def wait_for(ref, sem):
        pltpu.make_async_copy(ref, ref, sem).wait()

    load_cid = pltpu.make_async_copy(cid_hbm, cid_ref, cid_sem)
    load_cid.start()
    load = pltpu.make_async_copy(emb_hbm, emb, emb_sem)
    load.start()
    load_rank = pltpu.make_async_copy(rank_hbm, rank_ref, rank_sem)
    load_rank.start()
    barrier = pltpu.get_barrier_semaphore()
    for offset in range(1, ZS):
        pl.semaphore_signal(barrier, inc=1, device_id=z_peer(offset), device_id_type=MESH)
    for r in range(1, PLANE):
        pl.semaphore_signal(barrier, inc=1, device_id=plane_peer(r), device_id_type=MESH)
    pl.semaphore_signal(barrier, inc=1, device_id=sibling, device_id_type=MESH)

    load_cid.wait()
    cid = cid_ref[...]
    cx, cz, cy = cid >> 5, (cid >> 2) & 7, cid & 3
    dz = (cz - z) & 7
    step = jnp.where(dz <= 4, 2 * dz - 1, 2 * (ZS - dz))
    step = jnp.where(dz == 0, 0, step)
    across = ((cx - x) & 3) * YS + ((cy - y) & 3)
    hot = lax.broadcasted_iota(i32, (ZS * PLANE, rows), 0) == step * PLANE + across
    hot_f = jnp.where(hot, 1.0, 0.0)
    onehot[...] = hot_f.astype(bf16)
    upper = lax.broadcasted_iota(i32, (rows, rows), 0) < lax.broadcasted_iota(i32, (rows, rows), 1)
    before = jnp.dot(onehot[...], jnp.where(upper, 1.0, 0.0).astype(bf16), preferred_element_type=f32)
    place = jnp.sum(hot_f * before, axis=0, keepdims=True).astype(i32)
    lane = across * CAP + place
    slot = step * BLOCK + lane
    at_lane = lax.broadcasted_iota(i32, (128, rows), 0) == lane
    at_step = lax.broadcasted_iota(i32, (ZS, rows), 0) == step
    step_hot = jnp.where(at_step, 1.0, 0.0).astype(bf16)
    group = lax.broadcasted_iota(i32, (1, 128), 1) // CAP

    load.wait()
    wide = emb[...].astype(f32)
    scale = lax.rsqrt(jnp.sum(wide * wide, axis=1, keepdims=True) + 1e-06)
    normed[...] = (wide * scale).astype(bf16)

    def place_rows(first, count):
        span = count * BLOCK
        ids = lax.broadcasted_iota(i32, (span, rows), 0) + first * BLOCK
        pick = jnp.where(ids == slot, 1.0, 0.0).astype(bf16)
        placed = jnp.dot(pick, normed[...], preferred_element_type=f32)
        placed = placed.reshape(count * PLANE, CAP, width)
        paired = jnp.concatenate([placed[:, :, :half], placed[:, :, half:]], axis=1)
        snd[first : first + count] = paired.astype(bf16).reshape(count, PLANE, 2 * CAP, half)

    def source(j):
        return snd if j == 0 else zrcv

    def send_z(u):
        j, lo, hi = UNITS[u]
        some = pl.ds(lo, hi - lo)
        src = early.at[j - EARLY, some] if j >= EARLY else snd.at[j, some]
        send(src, zrcv.at[j, some], z_send, z_recv.at[u], z_peer(Z_OFFSETS[j]))

    def send_early(j):
        early[j - EARLY, 0] = snd[j, 0]
        for r in range(1, PLANE):
            send(snd.at[j, r], early.at[j - EARLY, r], e_send, e_recv.at[j - EARLY], plane_peer(r))

    def early_here(j):
        wait_for(early.at[j - EARLY, pl.ds(1, PLANE - 1)], e_recv.at[j - EARLY])

    def send_plane(u):
        j, lo, hi = UNITS[u]
        for r in range(max(lo, 1), hi):
            send(source(j).at[j, r], prcv.at[j, r], p_send, p_recv.at[u], plane_peer(r))

    def rank_along():
        load_rank.wait()
        number = rank_ref[...] + 1
        table = jnp.zeros((ZS, 128), f32)
        for shift in (0, 6, 12):
            digit = ((number >> shift) & 63).astype(f32)
            spread = jnp.where(at_lane, digit, 0.0).astype(bf16)
            table += contract_last(step_hot, spread) * float(1 << shift)
        for j in range(ZS):
            rsnd[j] = table[j : j + 1]
        for j in range(1, ZS):
            send(rsnd.at[j], zrk.at[j], r1_send, r1_recv, z_peer(Z_OFFSETS[j]))

    def rank_within():
        wait_for(zrk.at[pl.ds(1, ZS - 1)], r1_recv)
        rmid[...] = jnp.concatenate([rsnd[0]] + [zrk[j] for j in range(1, ZS)], axis=0)
        for r in range(1, PLANE):
            send(rmid, prk.at[r], r2_send, r2_recv, plane_peer(r))

    def spread_ranks(ranks, base):
        for j in range(ZS):
            key_rank[base + j] = jnp.transpose(jnp.broadcast_to(ranks[j], (BLOCK, BLOCK)))

    def rank_done():
        wait_for(prk.at[pl.ds(1, PLANE - 1)], r2_recv)
        found = rmid[...]
        for r in range(1, PLANE):
            found = jnp.where(group == r, prk[r], found)
        found = jnp.where(found == 0.0, BEYOND, found - 1.0)
        for j in range(ZS):
            rown[j] = found[j : j + 1]
        send(rown, rsib, r3_send, r3_recv, sibling)
        spread_ranks(rown, 0)

    def rank_sibling():
        wait_for(rsib, r3_recv)
        spread_ranks(rsib, ZS)

    def hand_over(u):
        j, lo, hi = UNITS[u]
        if j >= EARLY:
            wait_for(zrcv.at[j, pl.ds(lo, hi - lo)], z_recv.at[u])
            block = zrcv[j, lo:hi]
        else:
            wait_for(prcv.at[j, pl.ds(1, PLANE - 1)], p_recv.at[j])
            block = jnp.concatenate([source(j)[j, 0:1], prcv[j, 1:]], axis=0)
        block = block.astype(f32)
        size = (hi - lo) * CAP
        low = block[:, :CAP, :].reshape(size, half)
        high = block[:, CAP:, :].reshape(size, half)
        own[j, lo * CAP : hi * CAP] = jnp.concatenate([low, high], axis=1).astype(bf16)
        some = pl.ds(lo * CAP, size)
        send(own.at[j, some], sib.at[j, some], s_send, s_recv.at[u], sibling)

    def score(keys, ranks, queries):
        first, count = queries
        wanted = own[first : first + count].reshape(count * BLOCK, width)
        scores = contract_last(keys, wanted)
        for i in range(count):
            part = scores[:, i * BLOCK : (i + 1) * BLOCK]
            part = jnp.where(ranks < rown[first + i], part, -1.0)
            best = jnp.max(part.reshape(-1, 8, BLOCK), axis=0)
            acc[first + i] = jnp.maximum(acc[first + i], best)

    def keys_of(j, lo, hi):
        span = slice(lo * CAP, hi * CAP)
        keys = jnp.concatenate([own[j, span], sib[j, span]], axis=0)
        ranks = jnp.concatenate([key_rank[j, span], key_rank[ZS + j, span]], axis=0)
        return keys, ranks

    def new_keys(u, steps, then=None):
        j, lo, hi = UNITS[u]
        wait_for(sib.at[j, pl.ds(lo * CAP, (hi - lo) * CAP)], s_recv.at[u])
        keys, ranks = keys_of(j, lo, hi)
        for i in reversed(range(0, steps, 2)):
            score(keys, ranks, (i, min(2, steps - i)))
            if then is not None:
                then(i)

    def new_queries(j):
        for k in range(j):
            score(*keys_of(k, 0, PLANE), (j, 1))

    def scores_of(u):
        new_keys(u, u + 1)
        new_queries(u)

    place_rows(1, 1)
    pl.semaphore_wait(barrier, ZS - 1 + PLANE - 1 + 1)
    send_z(1)
    place_rows(2, 1)
    send_z(2)
    rank_along()
    place_rows(3, 2)
    send_z(3)
    send_z(4)
    place_rows(5, 2)
    send_early(5)
    send_early(6)
    place_rows(7, 1)
    send_early(7)
    place_rows(0, 1)
    send_plane(0)
    acc[...] = jnp.full(acc.shape, -1.0, f32)

    def pass_on(u):
        wait_for(zrcv.at[u], z_recv.at[u])
        send_plane(u)

    pass_on(1)
    pass_on(2)
    early_here(5)
    send_z(5)
    early_here(6)
    send_z(6)
    early_here(7)
    send_z(7)
    send_z(8)
    rank_within()
    for u in range(3):
        hand_over(u)
    rank_done()
    pass_on(3)
    pass_on(4)
    rank_sibling()
    for u in range(3):
        scores_of(u)
    hand_over(3)
    hand_over(4)
    scores_of(3)
    scores_of(4)
    hand_over(5)
    hand_over(6)
    scores_of(5)
    scores_of(6)
    hand_over(7)
    hand_over(8)
    new_queries(LAST)
    new_keys(7, ZS)

    def give_back(first):
        for j in (first, first + 1):
            res[j] = jnp.max(acc[j], axis=0, keepdims=True)
        for j, r in RETURNS:
            if j in (first, first + 1):
                send(res.at[j], fin.at[j * PLANE + r], o_send, o_recv, origin(j, r))

    new_keys(8, ZS, give_back)

    fin[0] = res[0]
    place_of = jnp.where(at_lane, 1.0, 0.0).astype(bf16)
    wait_for(fin.at[pl.ds(1, ZS * PLANE - 1)], o_recv)
    lines = []
    for j in range(ZS):
        line = jnp.zeros((1, 128), f32)
        for r in range(PLANE):
            line = jnp.where(group == r, fin[j * PLANE + r], line)
        lines.append(line)
    back = jnp.concatenate(lines, axis=0)
    parts = []
    for _ in range(3):
        parts.append(back.astype(bf16))
        back = back - parts[-1].astype(f32)
    parts = jnp.dot(jnp.concatenate(parts, axis=0), place_of, preferred_element_type=f32)
    total = parts[:ZS] + parts[ZS : 2 * ZS] + parts[2 * ZS :]
    out_ref[...] = jnp.sum(jnp.where(at_step, total, 0.0), axis=0, keepdims=True)

    wait_for(snd.at[pl.ds(1, ZS - 1)], z_send)
    wait_for(prcv.at[:, pl.ds(1, PLANE - 1)], p_send)
    wait_for(early.at[:, pl.ds(1, PLANE - 1)], e_send)
    wait_for(own, s_send)
    wait_for(zrk.at[pl.ds(1, ZS - 1)], r1_send)
    wait_for(prk.at[pl.ds(1, PLANE - 1)], r2_send)
    wait_for(rown, r3_send)
    wait_for(fin.at[pl.ds(1, ZS * PLANE - 1)], o_send)


def body(embeddings, cluster_id, rank):
    rows, width = embeddings.shape
    half = width // 2
    blocks = (ZS, PLANE, 2 * CAP, half)
    vmem = pltpu.VMEM
    dma = pltpu.SemaphoreType.DMA
    out = pl.pallas_call(
        kernel,
        out_shape=jax.ShapeDtypeStruct((1, rows), f32),
        in_specs=[pl.BlockSpec(memory_space=pltpu.HBM)] * 3,
        out_specs=pl.BlockSpec(memory_space=vmem),
        scratch_shapes=[
            vmem((rows, width), bf16),
            vmem((1, rows), i32),
            vmem((1, rows), i32),
            vmem((rows, width), bf16),
            vmem((ZS * PLANE, rows), bf16),
            vmem(blocks, bf16),
            vmem((ZS - EARLY,) + blocks[1:], bf16),
            vmem(blocks, bf16),
            vmem((EARLY,) + blocks[1:], bf16),
            vmem((ZS, BLOCK, width), bf16),
            vmem((ZS, BLOCK, width), bf16),
            vmem((ZS, 1, 128), f32),
            vmem((ZS, 1, 128), f32),
            vmem((ZS, 128), f32),
            vmem((PLANE, ZS, 128), f32),
            vmem((ZS, 1, 128), f32),
            vmem((ZS, 1, 128), f32),
            vmem((2 * ZS, BLOCK, BLOCK), f32),
            vmem((ZS, 8, BLOCK), f32),
            vmem((ZS, 1, 128), f32),
            vmem((ZS * PLANE, 1, 128), f32),
            dma, dma, dma, dma, dma((len(UNITS),)), dma, dma((EARLY,)), dma, dma((ZS - EARLY,)), dma, dma((len(UNITS),)),
            dma, dma, dma, dma, dma, dma, dma, dma,
        ],
        compiler_params=pltpu.CompilerParams(
            collective_id=0, has_side_effects=True, vmem_limit_bytes=62 << 20
        ),
        name="exchange_and_score",
    )(embeddings, cluster_id.reshape(1, rows), rank.reshape(1, rows))
    return out.reshape(rows)


def solution(mesh):
    in_specs = (P(("ingest", "span"), None), P(("ingest", "span")), P(("ingest", "span")))
    out_specs = P(("ingest", "span"))
    return jax.shard_map(body, mesh=mesh, in_specs=in_specs, out_specs=out_specs, check_vma=False)
```

```python
import jax
import jax.numpy as jnp
from jax import lax
from jax.experimental import pallas as pl
from jax.experimental.pallas import tpu as pltpu
from jax.sharding import PartitionSpec as P

XS, ZS, YS = 4, 8, 4
PLANE = XS * YS
CAP = 8
BLOCK = PLANE * CAP
BEYOND = float(2**30)
MESH = pl.DeviceIdType.MESH
Z_OFFSETS = (0, 1, 7, 2, 6, 3, 5, 4)
LAST = ZS - 1
EARLY = 5
UNITS = tuple((j, 0, PLANE) for j in range(ZS - 1)) + ((ZS - 1, 0, 12), (ZS - 1, 12, PLANE))


def distance(step, r):
    dx, dz, dy = r // YS, Z_OFFSETS[step], r % YS
    return min(dx, XS - dx) + min(dz, ZS - dz) + min(dy, YS - dy)


RETURNS = sorted(
    ((j, r) for j in range(ZS) for r in range(PLANE) if (j, r) != (0, 0)), key=lambda jr: -distance(*jr)
)
f32, bf16, i32 = jnp.float32, jnp.bfloat16, jnp.int32


def contract_last(a, b):
    return lax.dot_general(a, b, (((1,), (1,)), ((), ())), preferred_element_type=f32)


def kernel(
    emb_hbm, cid_hbm, rank_hbm, out_ref,
    emb, cid_ref, rank_ref, normed, onehot, snd, early, zrcv, prcv, own, sib,
    rsnd, zrk, rmid, prk, rown, rsib, key_rank, acc, res, fin,
    emb_sem, cid_sem, rank_sem, z_send, z_recv, p_send, p_recv, e_send, e_recv, s_send, s_recv,
    r1_send, r1_recv, r2_send, r2_recv, r3_send, r3_recv, o_send, o_recv,
):
    rows = cid_ref.shape[1]
    width = emb.shape[1]
    half = width // 2
    me = lax.axis_index("ingest")
    core = lax.axis_index("span")
    x, z, y = me // (ZS * YS), (me // YS) % ZS, me % YS

    def chip(px, pz, py):
        return (px * ZS + pz) * YS + py

    xs = [lax.rem(x + d, XS) for d in range(XS)]
    zs = [lax.rem(z + d, ZS) for d in range(ZS)]
    ys = [lax.rem(y + d, YS) for d in range(YS)]

    def z_peer(offset):
        return (chip(x, zs[offset], y), core)

    def plane_peer(r):
        return (chip(xs[r // YS], z, ys[r % YS]), core)

    def origin(j, r):
        return (chip(xs[-(r // YS) % XS], zs[-Z_OFFSETS[j] % ZS], ys[-(r % YS) % YS]), core)

    sibling = (me, 1 - core)

    def send(src, dst, send_sem, recv_sem, device):
        pltpu.make_async_remote_copy(
            src_ref=src, dst_ref=dst, send_sem=send_sem, recv_sem=recv_sem,
            device_id=device, device_id_type=MESH,
        ).start()

    def wait_for(ref, sem):
        pltpu.make_async_copy(ref, ref, sem).wait()

    load_cid = pltpu.make_async_copy(cid_hbm, cid_ref, cid_sem)
    load_cid.start()
    load = pltpu.make_async_copy(emb_hbm, emb, emb_sem)
    load.start()
    load_rank = pltpu.make_async_copy(rank_hbm, rank_ref, rank_sem)
    load_rank.start()
    barrier = pltpu.get_barrier_semaphore()
    for offset in range(1, ZS):
        pl.semaphore_signal(barrier, inc=1, device_id=z_peer(offset), device_id_type=MESH)
    for r in range(1, PLANE):
        pl.semaphore_signal(barrier, inc=1, device_id=plane_peer(r), device_id_type=MESH)
    pl.semaphore_signal(barrier, inc=1, device_id=sibling, device_id_type=MESH)

    load_cid.wait()
    cid = cid_ref[...]
    cx, cz, cy = cid >> 5, (cid >> 2) & 7, cid & 3
    dz = (cz - z) & 7
    step = jnp.where(dz <= 4, 2 * dz - 1, 2 * (ZS - dz))
    step = jnp.where(dz == 0, 0, step)
    across = ((cx - x) & 3) * YS + ((cy - y) & 3)
    hot = lax.broadcasted_iota(i32, (ZS * PLANE, rows), 0) == step * PLANE + across
    hot_f = jnp.where(hot, 1.0, 0.0)
    onehot[...] = hot_f.astype(bf16)
    upper = lax.broadcasted_iota(i32, (rows, rows), 0) < lax.broadcasted_iota(i32, (rows, rows), 1)
    before = jnp.dot(onehot[...], jnp.where(upper, 1.0, 0.0).astype(bf16), preferred_element_type=f32)
    place = jnp.sum(hot_f * before, axis=0, keepdims=True).astype(i32)
    lane = across * CAP + place
    slot = step * BLOCK + lane
    at_lane = lax.broadcasted_iota(i32, (128, rows), 0) == lane
    at_step = lax.broadcasted_iota(i32, (ZS, rows), 0) == step
    step_hot = jnp.where(at_step, 1.0, 0.0).astype(bf16)
    group = lax.broadcasted_iota(i32, (1, 128), 1) // CAP

    load.wait()
    wide = emb[...].astype(f32)
    scale = lax.rsqrt(jnp.sum(wide * wide, axis=1, keepdims=True) + 1e-06)
    normed[...] = (wide * scale).astype(bf16)

    def place_rows(first, count):
        span = count * BLOCK
        ids = lax.broadcasted_iota(i32, (span, rows), 0) + first * BLOCK
        pick = jnp.where(ids == slot, 1.0, 0.0).astype(bf16)
        placed = jnp.dot(pick, normed[...], preferred_element_type=f32)
        placed = placed.reshape(count * PLANE, CAP, width)
        paired = jnp.concatenate([placed[:, :, :half], placed[:, :, half:]], axis=1)
        snd[first : first + count] = paired.astype(bf16).reshape(count, PLANE, 2 * CAP, half)

    def source(j):
        return snd if j == 0 else zrcv

    def send_z(u):
        j, lo, hi = UNITS[u]
        some = pl.ds(lo, hi - lo)
        src = early.at[j - EARLY, some] if j >= EARLY else snd.at[j, some]
        send(src, zrcv.at[j, some], z_send, z_recv.at[u], z_peer(Z_OFFSETS[j]))

    def send_early(j):
        early[j - EARLY, 0] = snd[j, 0]
        for r in range(1, PLANE):
            send(snd.at[j, r], early.at[j - EARLY, r], e_send, e_recv.at[j - EARLY], plane_peer(r))

    def early_here(j):
        wait_for(early.at[j - EARLY, pl.ds(1, PLANE - 1)], e_recv.at[j - EARLY])

    def send_plane(u):
        j, lo, hi = UNITS[u]
        for r in range(max(lo, 1), hi):
            send(source(j).at[j, r], prcv.at[j, r], p_send, p_recv.at[u], plane_peer(r))

    def rank_along():
        load_rank.wait()
        number = rank_ref[...] + 1
        table = jnp.zeros((ZS, 128), f32)
        for shift in (0, 6, 12):
            digit = ((number >> shift) & 63).astype(f32)
            spread = jnp.where(at_lane, digit, 0.0).astype(bf16)
            table += contract_last(step_hot, spread) * float(1 << shift)
        for j in range(ZS):
            rsnd[j] = table[j : j + 1]
        for j in range(1, ZS):
            send(rsnd.at[j], zrk.at[j], r1_send, r1_recv, z_peer(Z_OFFSETS[j]))

    def rank_within():
        wait_for(zrk.at[pl.ds(1, ZS - 1)], r1_recv)
        rmid[...] = jnp.concatenate([rsnd[0]] + [zrk[j] for j in range(1, ZS)], axis=0)
        for r in range(1, PLANE):
            send(rmid, prk.at[r], r2_send, r2_recv, plane_peer(r))

    def spread_ranks(ranks, base):
        for j in range(ZS):
            key_rank[base + j] = jnp.transpose(jnp.broadcast_to(ranks[j], (BLOCK, BLOCK)))

    def rank_done():
        wait_for(prk.at[pl.ds(1, PLANE - 1)], r2_recv)
        found = rmid[...]
        for r in range(1, PLANE):
            found = jnp.where(group == r, prk[r], found)
        found = jnp.where(found == 0.0, BEYOND, found - 1.0)
        for j in range(ZS):
            rown[j] = found[j : j + 1]
        send(rown, rsib, r3_send, r3_recv, sibling)
        spread_ranks(rown, 0)

    def rank_sibling():
        wait_for(rsib, r3_recv)
        spread_ranks(rsib, ZS)

    def hand_over(u):
        j, lo, hi = UNITS[u]
        if j >= EARLY:
            wait_for(zrcv.at[j, pl.ds(lo, hi - lo)], z_recv.at[u])
            block = zrcv[j, lo:hi]
        else:
            wait_for(prcv.at[j, pl.ds(1, PLANE - 1)], p_recv.at[j])
            block = jnp.concatenate([source(j)[j, 0:1], prcv[j, 1:]], axis=0)
        block = block.astype(f32)
        size = (hi - lo) * CAP
        low = block[:, :CAP, :].reshape(size, half)
        high = block[:, CAP:, :].reshape(size, half)
        own[j, lo * CAP : hi * CAP] = jnp.concatenate([low, high], axis=1).astype(bf16)
        some = pl.ds(lo * CAP, size)
        send(own.at[j, some], sib.at[j, some], s_send, s_recv.at[u], sibling)

    def score(keys, ranks, queries):
        first, count = queries
        wanted = own[first : first + count].reshape(count * BLOCK, width)
        scores = contract_last(keys, wanted)
        for i in range(count):
            part = scores[:, i * BLOCK : (i + 1) * BLOCK]
            part = jnp.where(ranks < rown[first + i], part, -1.0)
            best = jnp.max(part.reshape(-1, 8, BLOCK), axis=0)
            acc[first + i] = jnp.maximum(acc[first + i], best)

    def keys_of(j, lo, hi):
        span = slice(lo * CAP, hi * CAP)
        keys = jnp.concatenate([own[j, span], sib[j, span]], axis=0)
        ranks = jnp.concatenate([key_rank[j, span], key_rank[ZS + j, span]], axis=0)
        return keys, ranks

    def new_keys(u, steps, then=None):
        j, lo, hi = UNITS[u]
        wait_for(sib.at[j, pl.ds(lo * CAP, (hi - lo) * CAP)], s_recv.at[u])
        keys, ranks = keys_of(j, lo, hi)
        for i in reversed(range(0, steps, 2)):
            score(keys, ranks, (i, min(2, steps - i)))
            if then is not None:
                then(i)

    def new_queries(j):
        for k in range(j):
            score(*keys_of(k, 0, PLANE), (j, 1))

    def scores_of(u):
        new_keys(u, u + 1)
        new_queries(u)

    place_rows(1, 1)
    pl.semaphore_wait(barrier, ZS - 1 + PLANE - 1 + 1)
    send_z(1)
    place_rows(2, 1)
    send_z(2)
    rank_along()
    place_rows(3, 2)
    send_z(3)
    send_z(4)
    place_rows(5, 2)
    send_early(5)
    send_early(6)
    place_rows(7, 1)
    send_early(7)
    place_rows(0, 1)
    send_plane(0)
    acc[...] = jnp.full(acc.shape, -1.0, f32)

    def pass_on(u):
        wait_for(zrcv.at[u], z_recv.at[u])
        send_plane(u)

    pass_on(1)
    pass_on(2)
    early_here(5)
    send_z(5)
    early_here(6)
    send_z(6)
    early_here(7)
    send_z(7)
    send_z(8)
    rank_within()
    for u in range(3):
        hand_over(u)
    rank_done()
    pass_on(3)
    pass_on(4)
    rank_sibling()
    for u in range(3):
        scores_of(u)
    hand_over(3)
    hand_over(4)
    scores_of(3)
    scores_of(4)
    hand_over(5)
    hand_over(6)
    scores_of(5)
    scores_of(6)
    hand_over(7)
    hand_over(8)
    new_queries(LAST)
    new_keys(7, ZS)

    def give_back(first):
        for j in (first, first + 1):
            res[j] = jnp.max(acc[j], axis=0, keepdims=True)
        for j, r in RETURNS:
            if j in (first, first + 1):
                send(res.at[j], fin.at[j * PLANE + r], o_send, o_recv, origin(j, r))

    new_keys(8, ZS, give_back)

    fin[0] = res[0]
    place_of = jnp.where(at_lane, 1.0, 0.0).astype(bf16)
    wait_for(fin.at[pl.ds(1, ZS * PLANE - 1)], o_recv)
    lines = []
    for j in range(ZS):
        line = jnp.zeros((1, 128), f32)
        for r in range(PLANE):
            line = jnp.where(group == r, fin[j * PLANE + r], line)
        lines.append(line)
    back = jnp.concatenate(lines, axis=0)
    parts = []
    for _ in range(3):
        parts.append(back.astype(bf16))
        back = back - parts[-1].astype(f32)
    parts = jnp.dot(jnp.concatenate(parts, axis=0), place_of, preferred_element_type=f32)
    total = parts[:ZS] + parts[ZS : 2 * ZS] + parts[2 * ZS :]
    out_ref[...] = jnp.sum(jnp.where(at_step, total, 0.0), axis=0, keepdims=True)

    wait_for(snd.at[pl.ds(1, ZS - 1)], z_send)
    wait_for(prcv.at[:, pl.ds(1, PLANE - 1)], p_send)
    wait_for(early.at[:, pl.ds(1, PLANE - 1)], e_send)
    wait_for(own, s_send)
    wait_for(zrk.at[pl.ds(1, ZS - 1)], r1_send)
    wait_for(prk.at[pl.ds(1, PLANE - 1)], r2_send)
    wait_for(rown, r3_send)
    wait_for(fin.at[pl.ds(1, ZS * PLANE - 1)], o_send)


def body(embeddings, cluster_id, rank):
    rows, width = embeddings.shape
    half = width // 2
    blocks = (ZS, PLANE, 2 * CAP, half)
    vmem = pltpu.VMEM
    dma = pltpu.SemaphoreType.DMA
    out = pl.pallas_call(
        kernel,
        out_shape=jax.ShapeDtypeStruct((1, rows), f32),
        in_specs=[pl.BlockSpec(memory_space=pltpu.HBM)] * 3,
        out_specs=pl.BlockSpec(memory_space=vmem),
        scratch_shapes=[
            vmem((rows, width), bf16),
            vmem((1, rows), i32),
            vmem((1, rows), i32),
            vmem((rows, width), bf16),
            vmem((ZS * PLANE, rows), bf16),
            vmem(blocks, bf16),
            vmem((ZS - EARLY,) + blocks[1:], bf16),
            vmem(blocks, bf16),
            vmem((EARLY,) + blocks[1:], bf16),
            vmem((ZS, BLOCK, width), bf16),
            vmem((ZS, BLOCK, width), bf16),
            vmem((ZS, 1, 128), f32),
            vmem((ZS, 1, 128), f32),
            vmem((ZS, 128), f32),
            vmem((PLANE, ZS, 128), f32),
            vmem((ZS, 1, 128), f32),
            vmem((ZS, 1, 128), f32),
            vmem((2 * ZS, BLOCK, BLOCK), f32),
            vmem((ZS, 8, BLOCK), f32),
            vmem((ZS, 1, 128), f32),
            vmem((ZS * PLANE, 1, 128), f32),
            dma, dma, dma, dma, dma((len(UNITS),)), dma, dma((EARLY,)), dma, dma((ZS - EARLY,)), dma, dma((len(UNITS),)),
            dma, dma, dma, dma, dma, dma, dma, dma,
        ],
        compiler_params=pltpu.CompilerParams(
            collective_id=0, has_side_effects=True, vmem_limit_bytes=62 << 20
        ),
        name="exchange_and_score",
    )(embeddings, cluster_id.reshape(1, rows), rank.reshape(1, rows))
    return out.reshape(rows)


def solution(mesh):
    in_specs = (P(("ingest", "span"), None), P(("ingest", "span")), P(("ingest", "span")))
    out_specs = P(("ingest", "span"))
    return jax.shard_map(body, mesh=mesh, in_specs=in_specs, out_specs=out_specs, check_vma=False)
```

```python
import jax
import jax.numpy as jnp
from jax import lax
from jax.experimental import pallas as pl
from jax.experimental.pallas import tpu as pltpu
from jax.sharding import PartitionSpec as P

XS, ZS, YS = 4, 8, 4
PLANE = XS * YS
CAP = 8
BLOCK = PLANE * CAP
BEYOND = float(2**30)
MESH = pl.DeviceIdType.MESH
Z_OFFSETS = (0, 1, 7, 2, 6, 3, 5, 4)
LAST = ZS - 1
EARLY = 5
UNITS = tuple((j, 0, PLANE) for j in range(ZS - 1)) + ((ZS - 1, 0, 12), (ZS - 1, 12, PLANE))


def distance(step, r):
    dx, dz, dy = r // YS, Z_OFFSETS[step], r % YS
    return min(dx, XS - dx) + min(dz, ZS - dz) + min(dy, YS - dy)


RETURNS = sorted(
    ((j, r) for j in range(ZS) for r in range(PLANE) if (j, r) != (0, 0)), key=lambda jr: -distance(*jr)
)
f32, bf16, i32 = jnp.float32, jnp.bfloat16, jnp.int32


def contract_last(a, b):
    return lax.dot_general(a, b, (((1,), (1,)), ((), ())), preferred_element_type=f32)


def kernel(
    emb_hbm, cid_hbm, rank_hbm, out_ref,
    emb, cid_ref, rank_ref, normed, onehot, snd, early, zrcv, prcv, own, sib,
    rsnd, zrk, rmid, prk, rown, rsib, key_rank, acc, earlier, res, fin,
    emb_sem, cid_sem, rank_sem, z_send, z_recv, p_send, p_recv, e_send, e_recv, s_send, s_recv,
    r1_send, r1_recv, r2_send, r2_recv, r3_send, r3_recv, o_send, o_recv,
):
    rows = cid_ref.shape[1]
    width = emb.shape[1]
    half = width // 2
    me = lax.axis_index("ingest")
    core = lax.axis_index("span")
    x, z, y = me // (ZS * YS), (me // YS) % ZS, me % YS

    def chip(px, pz, py):
        return (px * ZS + pz) * YS + py

    xs = [lax.rem(x + d, XS) for d in range(XS)]
    zs = [lax.rem(z + d, ZS) for d in range(ZS)]
    ys = [lax.rem(y + d, YS) for d in range(YS)]

    def z_peer(offset):
        return (chip(x, zs[offset], y), core)

    def plane_peer(r):
        return (chip(xs[r // YS], z, ys[r % YS]), core)

    def origin(j, r):
        return (chip(xs[-(r // YS) % XS], zs[-Z_OFFSETS[j] % ZS], ys[-(r % YS) % YS]), core)

    sibling = (me, 1 - core)

    def send(src, dst, send_sem, recv_sem, device):
        pltpu.make_async_remote_copy(
            src_ref=src, dst_ref=dst, send_sem=send_sem, recv_sem=recv_sem,
            device_id=device, device_id_type=MESH,
        ).start()

    def wait_for(ref, sem):
        pltpu.make_async_copy(ref, ref, sem).wait()

    load_cid = pltpu.make_async_copy(cid_hbm, cid_ref, cid_sem)
    load_cid.start()
    load = pltpu.make_async_copy(emb_hbm, emb, emb_sem)
    load.start()
    load_rank = pltpu.make_async_copy(rank_hbm, rank_ref, rank_sem)
    load_rank.start()
    barrier = pltpu.get_barrier_semaphore()
    for offset in range(1, ZS):
        pl.semaphore_signal(barrier, inc=1, device_id=z_peer(offset), device_id_type=MESH)
    for r in range(1, PLANE):
        pl.semaphore_signal(barrier, inc=1, device_id=plane_peer(r), device_id_type=MESH)
    pl.semaphore_signal(barrier, inc=1, device_id=sibling, device_id_type=MESH)

    upper = lax.broadcasted_iota(i32, (rows, rows), 0) < lax.broadcasted_iota(i32, (rows, rows), 1)
    earlier[...] = jnp.where(upper, 1.0, 0.0).astype(bf16)

    load_cid.wait()
    cid = cid_ref[...]
    cx, cz, cy = cid >> 5, (cid >> 2) & 7, cid & 3
    dz = (cz - z) & 7
    step = jnp.where(dz <= 4, 2 * dz - 1, 2 * (ZS - dz))
    step = jnp.where(dz == 0, 0, step)
    across = ((cx - x) & 3) * YS + ((cy - y) & 3)
    hot = lax.broadcasted_iota(i32, (ZS * PLANE, rows), 0) == step * PLANE + across
    hot_f = jnp.where(hot, 1.0, 0.0)
    onehot[...] = hot_f.astype(bf16)
    before = jnp.dot(onehot[...], earlier[...], preferred_element_type=f32)
    place = jnp.sum(hot_f * before, axis=0, keepdims=True).astype(i32)
    lane = across * CAP + place
    slot = step * BLOCK + lane
    at_lane = lax.broadcasted_iota(i32, (128, rows), 0) == lane
    at_step = lax.broadcasted_iota(i32, (ZS, rows), 0) == step
    step_hot = jnp.where(at_step, 1.0, 0.0).astype(bf16)
    group = lax.broadcasted_iota(i32, (1, 128), 1) // CAP

    load.wait()
    wide = emb[...].astype(f32)
    scale = lax.rsqrt(jnp.sum(wide * wide, axis=1, keepdims=True) + 1e-06)
    normed[...] = (wide * scale).astype(bf16)

    def place_rows(first, count):
        span = count * BLOCK
        ids = lax.broadcasted_iota(i32, (span, rows), 0) + first * BLOCK
        pick = jnp.where(ids == slot, 1.0, 0.0).astype(bf16)
        placed = jnp.dot(pick, normed[...], preferred_element_type=f32)
        placed = placed.reshape(count * PLANE, CAP, width)
        paired = jnp.concatenate([placed[:, :, :half], placed[:, :, half:]], axis=1)
        snd[first : first + count] = paired.astype(bf16).reshape(count, PLANE, 2 * CAP, half)

    def source(j):
        return snd if j == 0 else zrcv

    def send_z(u):
        j, lo, hi = UNITS[u]
        some = pl.ds(lo, hi - lo)
        src = early.at[j - EARLY, some] if j >= EARLY else snd.at[j, some]
        send(src, zrcv.at[j, some], z_send, z_recv.at[u], z_peer(Z_OFFSETS[j]))

    def send_early(j):
        early[j - EARLY, 0] = snd[j, 0]
        for r in range(1, PLANE):
            send(snd.at[j, r], early.at[j - EARLY, r], e_send, e_recv.at[j - EARLY], plane_peer(r))

    def early_here(j):
        wait_for(early.at[j - EARLY, pl.ds(1, PLANE - 1)], e_recv.at[j - EARLY])

    def send_plane(u):
        j, lo, hi = UNITS[u]
        for r in range(max(lo, 1), hi):
            send(source(j).at[j, r], prcv.at[j, r], p_send, p_recv.at[u], plane_peer(r))

    def rank_along():
        load_rank.wait()
        number = rank_ref[...] + 1
        table = jnp.zeros((ZS, 128), f32)
        for shift in (0, 6, 12):
            digit = ((number >> shift) & 63).astype(f32)
            spread = jnp.where(at_lane, digit, 0.0).astype(bf16)
            table += contract_last(step_hot, spread) * float(1 << shift)
        for j in range(ZS):
            rsnd[j] = table[j : j + 1]
        for j in range(1, ZS):
            send(rsnd.at[j], zrk.at[j], r1_send, r1_recv, z_peer(Z_OFFSETS[j]))

    def rank_within():
        wait_for(zrk.at[pl.ds(1, ZS - 1)], r1_recv)
        rmid[...] = jnp.concatenate([rsnd[0]] + [zrk[j] for j in range(1, ZS)], axis=0)
        for r in range(1, PLANE):
            send(rmid, prk.at[r], r2_send, r2_recv, plane_peer(r))

    def spread_ranks(ranks, base):
        for j in range(ZS):
            key_rank[base + j] = jnp.transpose(jnp.broadcast_to(ranks[j], (BLOCK, BLOCK)))

    def rank_done():
        wait_for(prk.at[pl.ds(1, PLANE - 1)], r2_recv)
        found = rmid[...]
        for r in range(1, PLANE):
            found = jnp.where(group == r, prk[r], found)
        found = jnp.where(found == 0.0, BEYOND, found - 1.0)
        for j in range(ZS):
            rown[j] = found[j : j + 1]
        send(rown, rsib, r3_send, r3_recv, sibling)
        spread_ranks(rown, 0)

    def rank_sibling():
        wait_for(rsib, r3_recv)
        spread_ranks(rsib, ZS)

    def hand_over(u):
        j, lo, hi = UNITS[u]
        if j >= EARLY:
            wait_for(zrcv.at[j, pl.ds(lo, hi - lo)], z_recv.at[u])
            block = zrcv[j, lo:hi]
        else:
            wait_for(prcv.at[j, pl.ds(1, PLANE - 1)], p_recv.at[j])
            block = jnp.concatenate([source(j)[j, 0:1], prcv[j, 1:]], axis=0)
        block = block.astype(f32)
        size = (hi - lo) * CAP
        low = block[:, :CAP, :].reshape(size, half)
        high = block[:, CAP:, :].reshape(size, half)
        own[j, lo * CAP : hi * CAP] = jnp.concatenate([low, high], axis=1).astype(bf16)
        some = pl.ds(lo * CAP, size)
        send(own.at[j, some], sib.at[j, some], s_send, s_recv.at[u], sibling)

    def score(keys, ranks, queries):
        first, count = queries
        wanted = own[first : first + count].reshape(count * BLOCK, width)
        scores = contract_last(keys, wanted)
        for i in range(count):
            part = scores[:, i * BLOCK : (i + 1) * BLOCK]
            part = jnp.where(ranks < rown[first + i], part, -1.0)
            best = jnp.max(part.reshape(-1, 8, BLOCK), axis=0)
            acc[first + i] = jnp.maximum(acc[first + i], best)

    def keys_of(j, lo, hi):
        span = slice(lo * CAP, hi * CAP)
        keys = jnp.concatenate([own[j, span], sib[j, span]], axis=0)
        ranks = jnp.concatenate([key_rank[j, span], key_rank[ZS + j, span]], axis=0)
        return keys, ranks

    def new_keys(u, steps, then=None):
        j, lo, hi = UNITS[u]
        wait_for(sib.at[j, pl.ds(lo * CAP, (hi - lo) * CAP)], s_recv.at[u])
        keys, ranks = keys_of(j, lo, hi)
        for i in reversed(range(0, steps, 2)):
            score(keys, ranks, (i, min(2, steps - i)))
            if then is not None:
                then(i)

    def new_queries(j):
        for k in range(j):
            score(*keys_of(k, 0, PLANE), (j, 1))

    def scores_of(u):
        new_keys(u, u + 1)
        new_queries(u)

    place_rows(1, 1)
    pl.semaphore_wait(barrier, ZS - 1 + PLANE - 1 + 1)
    send_z(1)
    place_rows(2, 1)
    send_z(2)
    rank_along()
    place_rows(3, 2)
    send_z(3)
    send_z(4)
    place_rows(5, 2)
    send_early(5)
    send_early(6)
    place_rows(7, 1)
    send_early(7)
    place_rows(0, 1)
    send_plane(0)
    acc[...] = jnp.full(acc.shape, -1.0, f32)

    def pass_on(u):
        wait_for(zrcv.at[u], z_recv.at[u])
        send_plane(u)

    pass_on(1)
    pass_on(2)
    early_here(5)
    send_z(5)
    early_here(6)
    send_z(6)
    early_here(7)
    send_z(7)
    send_z(8)
    rank_within()
    for u in range(3):
        hand_over(u)
    rank_done()
    pass_on(3)
    pass_on(4)
    rank_sibling()
    for u in range(3):
        scores_of(u)
    hand_over(3)
    hand_over(4)
    scores_of(3)
    scores_of(4)
    hand_over(5)
    hand_over(6)
    scores_of(5)
    scores_of(6)
    hand_over(7)
    hand_over(8)
    new_queries(LAST)
    new_keys(7, ZS)

    def give_back(first):
        for j in (first, first + 1):
            res[j] = jnp.max(acc[j], axis=0, keepdims=True)
        for j, r in RETURNS:
            if j in (first, first + 1):
                send(res.at[j], fin.at[j * PLANE + r], o_send, o_recv, origin(j, r))

    new_keys(8, ZS, give_back)

    fin[0] = res[0]
    place_of = jnp.where(at_lane, 1.0, 0.0).astype(bf16)
    wait_for(fin.at[pl.ds(1, ZS * PLANE - 1)], o_recv)
    lines = []
    for j in range(ZS):
        line = jnp.zeros((1, 128), f32)
        for r in range(PLANE):
            line = jnp.where(group == r, fin[j * PLANE + r], line)
        lines.append(line)
    back = jnp.concatenate(lines, axis=0)
    parts = []
    for _ in range(3):
        parts.append(back.astype(bf16))
        back = back - parts[-1].astype(f32)
    parts = jnp.dot(jnp.concatenate(parts, axis=0), place_of, preferred_element_type=f32)
    total = parts[:ZS] + parts[ZS : 2 * ZS] + parts[2 * ZS :]
    out_ref[...] = jnp.sum(jnp.where(at_step, total, 0.0), axis=0, keepdims=True)

    wait_for(snd.at[pl.ds(1, ZS - 1)], z_send)
    wait_for(prcv.at[:, pl.ds(1, PLANE - 1)], p_send)
    wait_for(early.at[:, pl.ds(1, PLANE - 1)], e_send)
    wait_for(own, s_send)
    wait_for(zrk.at[pl.ds(1, ZS - 1)], r1_send)
    wait_for(prk.at[pl.ds(1, PLANE - 1)], r2_send)
    wait_for(rown, r3_send)
    wait_for(fin.at[pl.ds(1, ZS * PLANE - 1)], o_send)


def body(embeddings, cluster_id, rank):
    rows, width = embeddings.shape
    half = width // 2
    blocks = (ZS, PLANE, 2 * CAP, half)
    vmem = pltpu.VMEM
    dma = pltpu.SemaphoreType.DMA
    out = pl.pallas_call(
        kernel,
        out_shape=jax.ShapeDtypeStruct((1, rows), f32),
        in_specs=[pl.BlockSpec(memory_space=pltpu.HBM)] * 3,
        out_specs=pl.BlockSpec(memory_space=vmem),
        scratch_shapes=[
            vmem((rows, width), bf16),
            vmem((1, rows), i32),
            vmem((1, rows), i32),
            vmem((rows, width), bf16),
            vmem((ZS * PLANE, rows), bf16),
            vmem(blocks, bf16),
            vmem((ZS - EARLY,) + blocks[1:], bf16),
            vmem(blocks, bf16),
            vmem((EARLY,) + blocks[1:], bf16),
            vmem((ZS, BLOCK, width), bf16),
            vmem((ZS, BLOCK, width), bf16),
            vmem((ZS, 1, 128), f32),
            vmem((ZS, 1, 128), f32),
            vmem((ZS, 128), f32),
            vmem((PLANE, ZS, 128), f32),
            vmem((ZS, 1, 128), f32),
            vmem((ZS, 1, 128), f32),
            vmem((2 * ZS, BLOCK, BLOCK), f32),
            vmem((ZS, 8, BLOCK), f32),
            vmem((rows, rows), bf16),
            vmem((ZS, 1, 128), f32),
            vmem((ZS * PLANE, 1, 128), f32),
            dma, dma, dma, dma, dma((len(UNITS),)), dma, dma((EARLY,)), dma, dma((ZS - EARLY,)), dma, dma((len(UNITS),)),
            dma, dma, dma, dma, dma, dma, dma, dma,
        ],
        compiler_params=pltpu.CompilerParams(
            collective_id=0, has_side_effects=True, vmem_limit_bytes=62 << 20
        ),
        name="exchange_and_score",
    )(embeddings, cluster_id.reshape(1, rows), rank.reshape(1, rows))
    return out.reshape(rows)


def solution(mesh):
    in_specs = (P(("ingest", "span"), None), P(("ingest", "span")), P(("ingest", "span")))
    out_specs = P(("ingest", "span"))
    return jax.shard_map(body, mesh=mesh, in_specs=in_specs, out_specs=out_specs, check_vma=False)
```
